32 devices in a mesh: row: 4 (over x, core), col: 8 (over z, y).
Axes of the slice: x: 2, y: 2, z: 4, core: 2. Of those that a mesh axis runs over, the one named last changes fastest.
Arguments:
- measured: float32 [16, 64, 1024], P(None, 'row', 'col')
- regions: int32 [4, 64], P('row', 'col'), may hold values from 0 to 63
- kernels: float32 [64, 9, 9], replicated, may hold values from 0 to 0.024691358
- radius: int32 [64], replicated, may hold values from 1 to 4, as said below
Outputs:
- solution: float32 [16, 64, 1024], P(None, 'row', 'col')
- residual: float32 [16, 64, 1024], P(None, 'row', 'col')
The draws below stay inside these ranges and needn't reach their ends.
Inputs may be any that keep to these rules, and one draw needn't show every extreme that they name: Some kernel has radius 4.
All inputs are finite; a program needn't handle non-finite values.
Results may differ from the reference program's by a relative error of at most 0.0029.
Values sent between devices are 32-bit elements; how exact they have to be, the bound alone decides.
No kernel may reach another device: no remote copies, remote signals or barrier semaphores. Data moves between devices by JAX's collectives and lax.ppermute only.
A program may use at most 64 MiB of HBM per device.

```python
import math
import jax
import jax.numpy as jnp
from jax import lax

FRAMES = 16
R = 4
K = 9
SUB = 16
REG = 64
ITERS = 3
NR = 64
NC = 1024


def draw_measured(key, part):
    key = jax.random.fold_in(key, 11)
    key_noise, key_frame, key_rough = jax.random.split(key, 3)
    row_pos = (jnp.arange(NR, dtype=jnp.float32) / NR)[:, None]
    col_pos = (jnp.arange(NC, dtype=jnp.float32) / NC)[None, :]
    frame_scale = jnp.exp(jax.random.uniform(key_frame, (FRAMES, 1, 1), jnp.float32, math.log(0.3), math.log(3.0)))
    rough_scale = jnp.exp(jax.random.uniform(key_rough, (NR, NC), jnp.float32, math.log(0.5), math.log(2.0)))
    base = jnp.clip(jax.random.normal(key_noise, (FRAMES, NR, NC), jnp.float32), -5.0, 5.0)
    ramp = 3.0 ** (row_pos + col_pos - 1.0)
    return (base * ramp * rough_scale * frame_scale).astype(jnp.float32)


def draw_radius(key, part):
    key = jax.random.fold_in(key, 7)
    key_base, key_pick = jax.random.split(key)
    base = jax.random.randint(key_base, (REG,), 1, R + 1)
    picked = jax.random.randint(key_pick, (), 0, REG)
    return jnp.where(jnp.arange(REG, dtype=jnp.int32) == picked, R, base).astype(jnp.int32)


def with_ends(drawn, rng, smallest, top_value):
    longest = drawn.shape.index(max(drawn.shape))
    spots = []
    for shift in (0, 1):
        where = [jax.random.randint(jax.random.fold_in(rng, axis), (), 0, length) for axis, length in enumerate(drawn.shape)]
        where[longest] = (where[longest] + shift) % drawn.shape[longest]
        spots.append(tuple(where))
    return drawn.at[spots[0]].set(smallest).at[spots[1]].set(top_value)


def setup_inputs(seed: int = 0) -> dict:
    seeds = jax.random.split(jax.random.key(seed), 5)
    return {
        "measured": draw_measured(jax.random.fold_in(seeds[4], 71), 0),
        "regions": with_ends(jax.random.randint(seeds[1], (NR // SUB, NC // SUB), 0, REG), jax.random.fold_in(seeds[1], 1), 0, REG - 1).astype(jnp.int32),
        "kernels": jnp.clip(jax.random.uniform(seeds[2], (REG, K, K), jnp.float32, 0.0, 0.024691358), 0.0, 0.024691358),
        "radius": draw_radius(jax.random.fold_in(seeds[4], 71), 0),
    }


DAMPING = 0.1

def tap_table(kernels, radius):
    offsets = jnp.arange(K, dtype=jnp.int32) - R
    reach_map = jnp.maximum(jnp.abs(offsets)[:, None], jnp.abs(offsets)[None, :])
    within = (reach_map[None, :, :] <= radius[:, None, None]).astype(kernels.dtype)
    return (kernels * within).reshape(REG, K * K)

def expand_grid(values):
    return jnp.repeat(jnp.repeat(values, SUB, axis=0), SUB, axis=1)

def forward_full(field, weight_grid):
    padded = jnp.pad(field, ((0, 0), (R, R), (R, R)))

    def accumulate(running, tap_index):
        shift_row = tap_index // K
        shift_col = tap_index % K
        zero_start = jnp.zeros((), jnp.int32)
        shifted = lax.dynamic_slice(padded, (zero_start, 2 * R - shift_row, 2 * R - shift_col), (FRAMES, NR, NC))
        upsampled = expand_grid(weight_grid[tap_index])
        return (running + upsampled * shifted, None)
    start = jnp.zeros((FRAMES, NR, NC), field.dtype)
    result, unused = lax.scan(accumulate, start, jnp.arange(K * K, dtype=jnp.int32))
    return result

def adjoint_full(values, weight_grid):

    def accumulate(running, tap_index):
        shift_row = tap_index // K
        shift_col = tap_index % K
        zero_start = jnp.zeros((), jnp.int32)
        weighted = values * expand_grid(weight_grid[tap_index])
        padded = jnp.pad(weighted, ((0, 0), (R, R), (R, R)))
        shifted = lax.dynamic_slice(padded, (zero_start, shift_row, shift_col), (FRAMES, NR, NC))
        return (running + shifted, None)
    start = jnp.zeros((FRAMES, NR, NC), values.dtype)
    result, unused = lax.scan(accumulate, start, jnp.arange(K * K, dtype=jnp.int32))
    return result

def apply_full(field, weight_grid):
    return adjoint_full(forward_full(field, weight_grid), weight_grid) + DAMPING * field

def gram_of(left, right):
    return jnp.einsum('fhw,ghw->fg', left, right, precision=lax.Precision.HIGHEST)

def combine(field, coefs):
    return jnp.einsum('fhw,fg->ghw', field, coefs, precision=lax.Precision.HIGHEST)

def solve_small(gram_matrix, right_side):
    lower = jnp.linalg.cholesky(gram_matrix)
    inner = lax.linalg.triangular_solve(lower, right_side, left_side=True, lower=True)
    return lax.linalg.triangular_solve(lower, inner, left_side=True, lower=True, transpose_a=True)

def reference(measured, regions, kernels, radius):
    tap_rows = tap_table(kernels, radius)
    weight_grid = jnp.moveaxis(tap_rows[regions], -1, 0)
    residual = adjoint_full(measured, weight_grid)
    solution = jnp.zeros_like(residual)
    direction = residual
    res_gram = gram_of(residual, residual)
    for iteration in range(ITERS):
        operated = apply_full(direction, weight_grid)
        curv_gram = gram_of(direction, operated)
        step_size = solve_small(curv_gram, res_gram)
        solution = solution + combine(direction, step_size)
        residual = residual - combine(operated, step_size)
        if iteration + 1 < ITERS:
            next_gram = gram_of(residual, residual)
            blend_coef = solve_small(res_gram, next_gram)
            direction = residual + combine(direction, blend_coef)
            res_gram = next_gram
    return (solution, residual)
```

```python
import functools

import jax
import jax.numpy as jnp
from jax import lax
from jax.experimental import pallas as pl
from jax.experimental.pallas import tpu as pltpu
from jax.sharding import PartitionSpec as P

R = 4
K = 9
SUB = 16
REG = 64
DAMPING = 0.1

LANES = 128
HALO = 32
PACK = LANES // HALO
NB = 4

F32 = jnp.float32
BF16 = jnp.bfloat16
NN = (((1,), (0,)), ((), ()))
NT = (((1,), (1,)), ((), ()))
HIGHEST = lax.Precision.HIGHEST
VMEM = pl.BlockSpec(memory_space=pltpu.VMEM)
SMEM = pl.BlockSpec(memory_space=pltpu.SMEM)
PARAMS = pltpu.CompilerParams(vmem_limit_bytes=48 << 20)


def split(value):
    high = value.astype(BF16)
    return high, (value - high.astype(F32)).astype(BF16)


def lane_iota(rows):
    return lax.broadcasted_iota(jnp.int32, (rows, LANES), 1)


def row_of(ref, index, row):
    frames, rows = ref.shape[1], ref.shape[2]
    flat = ref.reshape(ref.shape[0] * frames * rows, LANES)
    return flat[pl.ds(index * frames * rows + row, frames, stride=rows), :]


def pack_kernel(where_ref, labels_ref, *refs):
    tiles, out = refs[:-1], refs[-1]
    q = where_ref[1]
    slot = 0
    for tile in tiles:
        for index in range(tile.shape[0]):
            for group in range(SUB // PACK):
                packed = None
                for m in range(PACK):
                    line = row_of(tile, index, group * PACK + m)
                    line = pltpu.roll(line, HALO * m + HALO * q, 1)
                    lanes = lane_iota(line.shape[0])
                    packed = line if packed is None else jnp.where(lanes >= HALO * m, line, packed)
                out[slot] = packed
                slot += 1
    out[slot] = labels_ref[...]


def stage_weights(bt, s, transposed):
    zero = jnp.zeros((LANES, LANES), BF16)

    def block(a):
        return bt[s, a] if 0 <= a < K else zero

    blocks = []
    for t in range(5):
        if transposed:
            index = [[2 * t + i - o for o in range(2)] for i in range(2)]
        else:
            index = [[8 - 2 * t + o - i for i in range(2)] for o in range(2)]
        blocks.append(
            jnp.concatenate([jnp.concatenate([block(a) for a in line], 1) for line in index], 0)
        )
    return blocks


def main_kernel(
    rows, ntiles, nhalos, ndev, xor,
    where_ref, real_ref, labels_ref, table_ref, *refs,
):
    tiles, halos = refs[:ntiles], refs[ntiles : ntiles + nhalos]
    gram_ref, keep_ref, send_ref = refs[ntiles + nhalos : ntiles + nhalos + 3]
    bth, btl, base_ref, vh, vl, uh, ul, acc, kr = refs[ntiles + nhalos + 3 :]
    r, q, beside = where_ref[0], where_ref[1], where_ref[2]
    shift = real_ref[0]
    pairs = rows * SUB // 2
    lanes = lane_iota(16)

    def each(body):
        if rows <= 4:
            for s in range(rows):
                body(s)
        else:
            lax.fori_loop(0, rows, lambda s, c: (body(s), c)[1], 0)

    th, tl = split(table_ref[...])
    slots = []
    for ref in tiles:
        for index in range(ref.shape[0]):
            slots.append((ref, index))
    per_halo = rows // nhalos
    for k in range(rows):
        s = (r ^ k) if xor else k
        own = labels_ref[pl.ds(s, 1), :]
        halo = halos[k // per_halo]
        line = (k % per_halo)
        beside_labels = halo[per_halo * (SUB // PACK), line : line + 1, :]
        own = jnp.broadcast_to(own, (8, LANES))
        beside_labels = jnp.broadcast_to(beside_labels, (8, LANES))
        lanes8 = lane_iota(8)
        left = jnp.where(lanes8 < 2, pltpu.roll(beside_labels, LANES - 6, 1), pltpu.roll(own, 2, 1))
        right = jnp.where(lanes8 < 6, pltpu.roll(own, LANES - 2, 1), pltpu.roll(beside_labels, 6, 1))
        window = jnp.where(q == 0, left, right)
        diagonal = lanes8 == lax.broadcasted_iota(jnp.int32, (8, LANES), 0)
        column = jnp.sum(jnp.where(diagonal, window, 0.0), axis=1, keepdims=True)
        hot = (column == (lanes8[:, :REG] + 1).astype(F32)).astype(BF16)
        base_ref[k] = lax.dot_general(hot, th, NN, preferred_element_type=F32) + lax.dot_general(
            hot, tl, NN, preferred_element_type=F32
        )
    for k in range(rows):
        s = (r ^ k) if xor else k
        for a in range(K):
            for c in range(LANES // SUB):
                line = base_ref[k, c : c + 1, a * LANES : (a + 1) * LANES]
                band = pltpu.roll(
                    jnp.broadcast_to(line, (SUB, LANES)), SUB * c, 1, stride=1, stride_axis=0
                )
                high, low = split(band)
                bth[s, a, c * SUB : (c + 1) * SUB, :] = high
                btl[s, a, c * SUB : (c + 1) * SUB, :] = low

    blank = jnp.zeros((2, 16, 2 * LANES), BF16)
    for ref in (vh, vl, uh, ul):
        ref[0:2] = blank
        ref[pairs + 2 : pairs + 4] = blank
    edge_start = (LANES - HALO) * q
    in_halo = (lanes >= edge_start) & (lanes < edge_start + HALO)
    for k, (ref, index) in enumerate(slots):
        s = (r ^ k) if xor else k
        halo = halos[k // per_halo]
        for i in range(SUB):
            line = pltpu.roll(row_of(ref, index, i), HALO + (LANES - 2 * HALO) * q, 1)
            edge = halo[(k % per_halo) * (SUB // PACK) + i // PACK]
            edge = pltpu.roll(edge, (LANES - HALO * (i % PACK) + (LANES - HALO) * q) % LANES, 1)
            high, low = split(jnp.where(in_halo, edge, line))
            pair = 2 + s * (SUB // 2) + i // 2
            part = slice((i % 2) * LANES, (i % 2 + 1) * LANES)
            uh[pair, :, part] = high
            ul[pair, :, part] = low

    inside = jnp.where(in_halo, beside.astype(F32), 1.0)
    inside = jnp.concatenate([inside, inside], 1)

    def product(high, low, wh, wl, dims):
        both = lax.dot_general(
            jnp.concatenate([high, low], 0), wh, dims, preferred_element_type=F32
        )
        third = lax.dot_general(high, wl, dims, preferred_element_type=F32)
        return both[: high.shape[0]] + both[high.shape[0] :] + third

    def adjoint(n):
        acc[...] = jnp.zeros_like(acc)

        def body(s):
            wh, wl = stage_weights(bth, s, True), stage_weights(btl, s, True)
            start = s * 8
            high = uh[pl.ds(start + 2, 8)].reshape(128, 2 * LANES)
            low = ul[pl.ds(start + 2, 8)].reshape(128, 2 * LANES)
            for t in range(5):
                out = product(high, low, wh[t], wl[t], NN).reshape(8, 16, 2 * LANES)
                acc[pl.ds(start + 4 - t, 8)] += out

        each(body)

        def finish(s):
            start = s * 8
            value = acc[pl.ds(start + 2, 8)]
            if n > 0:
                value = value - shift * kr[n - 1, pl.ds(start, 8)]
            value = value * inside[None]
            kr[n, pl.ds(start, 8)] = value
            if n < NB - 1:
                high, low = split(value)
                vh[pl.ds(start + 2, 8)] = high
                vl[pl.ds(start + 2, 8)] = low

        each(finish)

    def forward():
        def body(s):
            wh, wl = stage_weights(bth, s, False), stage_weights(btl, s, False)
            start = s * 8
            total = None
            for t in range(5):
                high = vh[pl.ds(start + t, 8)].reshape(128, 2 * LANES)
                low = vl[pl.ds(start + t, 8)].reshape(128, 2 * LANES)
                out = product(high, low, wh[t], wl[t], NT)
                total = out if total is None else total + out
            high, low = split(total.reshape(8, 16, 2 * LANES))
            uh[pl.ds(start + 2, 8)] = high
            ul[pl.ds(start + 2, 8)] = low

        each(body)

    adjoint(0)
    for n in range(1, NB):
        forward()
        adjoint(n)

    first = lanes < LANES // 2
    for ref, row in ((keep_ref, r), (send_ref, r ^ 1)):
        for n in range(NB):
            for p in range(8):
                value = kr[n, row * 8 + p]
                ref[n, p] = jnp.where(
                    first,
                    pltpu.roll(value[:, :LANES], LANES - HALO, 1),
                    pltpu.roll(value[:, LANES:], HALO, 1),
                )
    gram = jnp.zeros((NB * 16, NB * 16), F32)
    for p in range(8):
        stack = jnp.concatenate(
            [
                jnp.concatenate([ref[n, p] for n in range(NB)], 0)
                for ref in (keep_ref, send_ref)
            ],
            1,
        )
        gram = gram + lax.dot_general(stack, stack, NT, precision=HIGHEST, preferred_element_type=F32)
    gram = jnp.concatenate([gram, jnp.zeros_like(gram)], 1)
    message = jnp.zeros((16, LANES), F32)
    for g in range(2 * NB - 2):
        i, j = g // 2, (g + 1) // 2
        part = pltpu.roll(gram[16 * i : 16 * i + 16], (16 * (g - j)) % LANES, 1)
        message = jnp.where((lanes >= 16 * g) & (lanes < 16 * g + 16), part, message)
    for dev in range(ndev):
        gram_ref[dev] = message


def final_kernel(ndev, where_ref, real_ref, gram_ref, keep_ref, other_ref, solution_ref, residual_ref):
    q = where_ref[1]
    damp = real_ref[1]
    parts = [gram_ref[dev] for dev in range(ndev)]
    while len(parts) > 1:
        parts = [a + b for a, b in zip(parts[::2], parts[1::2])]
    grams = parts[0]
    lanes = lane_iota(16)

    def at(g, place):
        moved = pltpu.roll(grams, (16 * (place - g)) % LANES, 1) if place != g else grams
        return moved

    lines = []
    for i in range(3):
        line = jnp.zeros((16, LANES), F32)
        for j in range(3):
            here = (lanes >= 16 * j) & (lanes < 16 * j + 16)
            line = jnp.where(here, at(i + j + 1, j) + damp * at(i + j, j), line)
        here = (lanes >= 48) & (lanes < 64)
        lines.append(jnp.where(here, at(i, 3), line))
    matrix = jnp.concatenate(lines, 0)
    place = lax.broadcasted_iota(jnp.int32, (48, 1), 0)
    for k in range(48):
        row = matrix[k : k + 1, :] / matrix[k : k + 1, k : k + 1]
        column = matrix[:, k : k + 1] - (place == k).astype(F32)
        matrix = matrix - column * row
    c = [pltpu.roll(matrix[16 * i : 16 * i + 16], LANES - 48, 1) for i in range(3)]
    eye = (lax.broadcasted_iota(jnp.int32, (16, LANES), 0) == lanes).astype(F32)
    zero = jnp.zeros((16, LANES), F32)
    in_solution = [0.5 * c[0], 0.5 * c[1], 0.5 * c[2], zero]
    in_residual = [
        2.0 * (eye - damp * c[0]),
        -2.0 * (c[0] + damp * c[1]),
        -2.0 * (c[1] + damp * c[2]),
        -2.0 * c[2],
    ]
    weights = jnp.concatenate(
        [jnp.where(lanes < 16, a, pltpu.roll(b, 16, 1)) for a, b in zip(in_solution, in_residual)], 0
    )
    weights = jnp.concatenate([weights, jnp.zeros_like(weights)], 0).T[:32, : NB * 16]
    first = lanes < LANES // 2
    first2 = jnp.concatenate([first, first], 0)
    outs = (
        solution_ref.reshape(16 * SUB, LANES),
        residual_ref.reshape(16 * SUB, LANES),
    )
    for p in range(8):
        mine = jnp.concatenate([keep_ref[n, p] for n in range(NB)], 0)
        pair = jnp.concatenate([other_ref[n, p] for n in range(NB)], 0)
        both = jnp.concatenate([mine, pair], 1)
        out = lax.dot_general(weights, both, NN, precision=HIGHEST, preferred_element_type=F32)
        a, b = out[:, :LANES], out[:, LANES:]
        left, right = jnp.where(q == 0, a, b), jnp.where(q == 0, b, a)
        even = jnp.where(first2, left, pltpu.roll(right, LANES // 2, 1))
        odd = jnp.where(first2, pltpu.roll(left, LANES // 2, 1), right)
        for o, ref in enumerate(outs):
            ref[pl.ds(2 * p, 16, stride=SUB), :] = even[16 * o : 16 * o + 16]
            ref[pl.ds(2 * p + 1, 16, stride=SUB), :] = odd[16 * o : 16 * o + 16]


def per_device(measured, regions, kernels, radius):
    nrow, ncol = lax.axis_size("row"), lax.axis_size("col")
    ndev = nrow * ncol
    r, c = lax.axis_index("row"), lax.axis_index("col")
    q = (r ^ c) & 1
    beside = jnp.where(q == 0, c > 0, c < ncol - 1).astype(jnp.int32)
    where = jnp.stack([r.astype(jnp.int32), q.astype(jnp.int32), beside])

    offsets = jnp.abs(jnp.arange(K, dtype=jnp.int32) - R)
    reach = jnp.maximum(offsets[:, None], offsets[None, :])
    taps = 0.5 * kernels * (reach[None] <= radius[:, None, None]).astype(F32)
    table = jnp.pad(taps[:, :, ::-1], ((0, 0), (0, 0), (0, LANES - K)))
    table = jnp.roll(table, -R, axis=2).reshape(REG, K * LANES)
    squares = jnp.sum(taps, (1, 2)) ** 2
    shift = 0.5 * jnp.sqrt(jnp.mean(squares) * jnp.max(squares))
    real = jnp.stack([shift, shift + 0.25 * DAMPING])

    def flip(value, bit):
        return lax.ppermute(value, "row", [(i, i ^ bit) for i in range(nrow)])

    facing = []
    for i in range(nrow):
        for j in range(ncol):
            other = j + (1 if (i ^ j) & 1 else -1)
            if 0 <= other < ncol:
                facing.append((i * ncol + j, i * ncol + other))

    def labels_of(value, height):
        return jnp.pad((value + 1).astype(F32), ((0, height - value.shape[0]), (0, LANES - value.shape[1])))

    everyone = lax.all_gather(regions, "row", axis=0, tiled=True)
    xor = nrow == 4
    if xor:
        mine = measured[None]
        pair = flip(mine, 1)
        tiles = [mine, pair]
        labels = labels_of(jnp.concatenate([regions, flip(regions, 1)], 0), 16)
    else:
        tiles = [lax.all_gather(measured, "row", axis=0)]
        labels = labels_of(everyone, 16)
    blocks = sum(t.shape[0] for t in tiles)
    edges = pl.pallas_call(
        pack_kernel,
        out_shape=jax.ShapeDtypeStruct((blocks * (SUB // PACK) + 1, 16, LANES), F32),
        in_specs=[SMEM] + [VMEM] * (1 + len(tiles)),
        out_specs=VMEM,
        compiler_params=PARAMS,
        name="pack",
    )(where, labels, *tiles)
    halos = [lax.ppermute(edges, ("row", "col"), facing)]
    if xor:
        far = flip(mine, 2)
        tiles += [far, flip(far, 1)]
        halos.append(flip(halos[0], 2))

    pairs = nrow * SUB // 2
    packed = jax.ShapeDtypeStruct((NB, 8, 16, LANES), F32)
    grams, keep, send = pl.pallas_call(
        functools.partial(main_kernel, nrow, len(tiles), len(halos), ndev, xor),
        out_shape=(jax.ShapeDtypeStruct((ndev, 16, LANES), F32), packed, packed),
        in_specs=[SMEM, SMEM] + [VMEM] * (2 + len(tiles) + len(halos)),
        out_specs=(VMEM, VMEM, VMEM),
        scratch_shapes=[pltpu.VMEM((nrow, K, LANES, LANES), BF16)] * 2
        + [pltpu.VMEM((nrow, 8, K * LANES), F32)]
        + [pltpu.VMEM((pairs + 4, 16, 2 * LANES), BF16)] * 4
        + [pltpu.VMEM((pairs + 4, 16, 2 * LANES), F32), pltpu.VMEM((NB, pairs, 16, 2 * LANES), F32)],
        compiler_params=PARAMS,
        name="krylov",
    )(where, real, labels_of(everyone, max(8, nrow)), table, *tiles, *halos)

    other = flip(send, 1)
    grams = lax.all_to_all(grams, ("row", "col"), 0, 0)
    tile = jax.ShapeDtypeStruct((16, SUB, LANES), F32)
    return pl.pallas_call(
        functools.partial(final_kernel, ndev),
        out_shape=(tile, tile),
        in_specs=[SMEM, SMEM] + [VMEM] * 3,
        out_specs=(VMEM, VMEM),
        compiler_params=PARAMS,
        name="combine",
    )(where, real, grams, keep, other)


def solution(mesh):
    in_specs = (P(None, "row", "col"), P("row", "col"), P(), P())
    out_specs = (P(None, "row", "col"), P(None, "row", "col"))
    return jax.shard_map(
        per_device, mesh=mesh, in_specs=in_specs, out_specs=out_specs, check_vma=False
    )
```

```python
import functools

import jax
import jax.numpy as jnp
from jax import lax
from jax.experimental import pallas as pl
from jax.experimental.pallas import tpu as pltpu
from jax.sharding import PartitionSpec as P

R = 4
K = 9
SUB = 16
REG = 64
DAMPING = 0.1

LANES = 128
HALO = 32
PACK = LANES // HALO
NB = 4

F32 = jnp.float32
BF16 = jnp.bfloat16
NN = (((1,), (0,)), ((), ()))
NT = (((1,), (1,)), ((), ()))
HIGHEST = lax.Precision.HIGHEST
VMEM = pl.BlockSpec(memory_space=pltpu.VMEM)
SMEM = pl.BlockSpec(memory_space=pltpu.SMEM)
def params(mib):
    return pltpu.CompilerParams(vmem_limit_bytes=mib << 20)


def split(value):
    high = value.astype(BF16)
    return high, (value - high.astype(F32)).astype(BF16)


def lane_iota(rows):
    return lax.broadcasted_iota(jnp.int32, (rows, LANES), 1)


def row_of(ref, index, row):
    frames, rows = ref.shape[1], ref.shape[2]
    flat = ref.reshape(ref.shape[0] * frames * rows, LANES)
    return flat[pl.ds(index * frames * rows + row, frames, stride=rows), :]


def place():
    r, c = lax.axis_index("row"), lax.axis_index("col")
    q = (r ^ c) & 1
    beside = jnp.where(q == 0, c > 0, c < lax.axis_size("col") - 1)
    return r, q, beside.astype(jnp.int32)


def pack_tile(tile, index, out, slot):
    q = place()[1]
    for group in range(SUB // PACK):
        packed = None
        for m in range(PACK):
            line = row_of(tile, index, group * PACK + m)
            line = pltpu.roll(line, HALO * m + HALO * q, 1)
            lanes = lane_iota(line.shape[0])
            packed = line if packed is None else jnp.where(lanes >= HALO * m, line, packed)
        out[slot + group] = packed


def first_kernel(tile, radius_ref, out, reach_ref):
    for index in range(tile.shape[0]):
        pack_tile(tile, index, out, index * (SUB // PACK))
    reach_ref[...] = jnp.zeros_like(reach_ref)
    reach_ref[0:1, :REG] = radius_ref[...]


def pack_kernel(nlabels, packed, *refs):
    labels, tiles, (out, tags) = refs[:nlabels], refs[nlabels:-2], refs[-2:]
    slot = packed.shape[0]
    out[:slot] = packed[...]
    for tile in tiles:
        pack_tile(tile, 0, out, slot)
        slot += SUB // PACK
    tags[...] = jnp.zeros((16, LANES), F32)
    line = 0
    for ref in labels:
        height, width = ref.shape
        tags[line : line + height, :width] = (ref[...] + 1).astype(F32)
        line += height
    out[slot] = tags[...]


def stage_weights(bt, s, transposed):
    zero = jnp.zeros((LANES, LANES), BF16)

    def block(a):
        return bt[s, a] if 0 <= a < K else zero

    blocks = []
    for t in range(5):
        if transposed:
            index = [[2 * t + i - o for o in range(2)] for i in range(2)]
        else:
            index = [[8 - 2 * t + o - i for i in range(2)] for o in range(2)]
        blocks.append(
            jnp.concatenate([jnp.concatenate([block(a) for a in line], 1) for line in index], 0)
        )
    return blocks


class Rows:
    def __init__(self, rows, xor):
        self.rows, self.xor = rows, xor
        self.r, self.q, self.beside = place()
        self.down = (self.r >> 1) if xor else 0
        lanes = lane_iota(16)
        start = (LANES - HALO) * self.q
        self.in_halo = (lanes >= start) & (lanes < start + HALO)

    def block(self, k):
        return (k & 2) + ((k ^ self.r ^ self.down) & 1) if self.xor else k

    def turn(self, i, last):
        return i + self.down * (last - 2 * i) if self.xor else i

    def each(self, body, count, first=0):
        if self.xor:
            for s in range(first, count):
                body(s)
        else:
            lax.fori_loop(0, self.rows, lambda s, c: (body(s), c)[1], 0)

    def inside(self):
        mask = jnp.where(self.in_halo, self.beside.astype(F32), 1.0)
        return jnp.concatenate([mask, mask], 1)

    def own(self):
        return (self.block(0), self.block(1)) if self.xor else (self.r, self.r ^ 1)


def tables(taps_ref, radius_ref):
    radius = radius_ref[0:1, :REG]
    high, low, total = [], [], jnp.zeros((1, REG), F32)
    b = lax.broadcasted_iota(jnp.int32, (K, REG), 0)
    for a in range(K):
        reach = jnp.maximum(jnp.abs(b - R), abs(a - R))
        taps = jnp.where(reach <= radius, 0.5 * taps_ref[a], 0.0)
        total = total + jnp.sum(taps, axis=0, keepdims=True)
        for part, value in zip((high, low), split(taps)):
            part.append(value)
    squares = total * total
    mean = jnp.sum(squares, axis=1, keepdims=True) * (1.0 / REG)
    return high, low, 0.5 * jnp.sqrt(mean * jnp.max(squares, axis=1, keepdims=True))


def make_bands(where, blocks, high, low, labels, halo, base_ref, bth, btl):
    lanes = lane_iota(8)
    count = len(blocks)
    hots = []
    for j in range(count):
        own = jnp.broadcast_to(labels[j], (8, LANES))
        beside = jnp.broadcast_to(halo[count * (SUB // PACK) + j // 16, j % 16 : j % 16 + 1, :], (8, LANES))
        left = jnp.where(lanes < 2, pltpu.roll(beside, LANES - 6, 1), pltpu.roll(own, 2, 1))
        right = jnp.where(lanes < 6, pltpu.roll(own, LANES - 2, 1), pltpu.roll(beside, 6, 1))
        window = jnp.where(where.q == 0, left, right)
        diagonal = lanes == lax.broadcasted_iota(jnp.int32, (8, LANES), 0)
        column = jnp.sum(jnp.where(diagonal, window, 0.0), axis=1, keepdims=True)
        hots.append((column == (lanes[:, :REG] + 1).astype(F32)).astype(F32))
    hot = jnp.concatenate(hots, 0).astype(BF16)
    b = lax.broadcasted_iota(jnp.int32, (K, LANES), 0)
    spread = (lax.broadcasted_iota(jnp.int32, (K, LANES), 1) == (LANES + R - b) % LANES).astype(BF16)
    for a in range(K):
        base = None
        for part in (high, low):
            picked = lax.dot_general(hot, part[a], NT, preferred_element_type=F32).astype(BF16)
            line = lax.dot_general(picked, spread, NN, preferred_element_type=F32)
            base = line if base is None else base + line
        for j in range(count):
            base_ref[j, a] = base[8 * j : 8 * j + 8]
    for j, s in enumerate(blocks):
        for a in range(K):
            squares = base_ref[j, where.turn(a, K - 1)]
            for c in range(LANES // SUB):
                band = jnp.broadcast_to(squares[c : c + 1], (SUB, LANES))
                band = pltpu.roll(band, SUB * c, 1, stride=1, stride_axis=0)
                for ref, value in zip((bth, btl), split(band)):
                    ref[s, a, c * SUB : (c + 1) * SUB, :] = value


def make_window(where, blocks, tiles, halo, uh, ul):
    for j, (s, (ref, index)) in enumerate(zip(blocks, tiles)):
        for p in range(SUB // 2):
            parts = []
            for i in (where.turn(2 * p, SUB - 1), where.turn(2 * p + 1, SUB - 1)):
                line = pltpu.roll(row_of(ref, index, i), HALO + (LANES - 2 * HALO) * where.q, 1)
                edge = halo[j * (SUB // PACK) + i // PACK]
                edge = pltpu.roll(edge, (LANES - HALO * (i % PACK) + (LANES - HALO) * where.q) % LANES, 1)
                parts.append(jnp.where(where.in_halo, edge, line))
            for out, value in zip((uh, ul), split(jnp.concatenate(parts, 1))):
                out[s * (SUB // 2) + p] = value


def product(high, low, wh, wl, dims):
    both = lax.dot_general(jnp.concatenate([high, low], 0), wh, dims, preferred_element_type=F32)
    third = lax.dot_general(high, wl, dims, preferred_element_type=F32)
    return both[: high.shape[0]] + both[high.shape[0] :] + third


def spread_rows(bands, uh, ul, base, acc, s):
    wh, wl = (stage_weights(*bands(s, i), True) for i in range(2))
    start = (s - base) * 8
    high = uh[pl.ds(start, 8)].reshape(128, 2 * LANES)
    low = ul[pl.ds(start, 8)].reshape(128, 2 * LANES)
    for t in range(5):
        out = product(high, low, wh[t], wl[t], NN).reshape(8, 16, 2 * LANES)
        acc[pl.ds(s * 8 + 4 - t, 8)] += out


def gather_rows(bands, vh, vl, s):
    wh, wl = (stage_weights(*bands(s, i), False) for i in range(2))
    total = None
    for t in range(5):
        high = vh[pl.ds(s * 8 + t, 8)].reshape(128, 2 * LANES)
        low = vl[pl.ds(s * 8 + t, 8)].reshape(128, 2 * LANES)
        out = product(high, low, wh[t], wl[t], NT)
        total = out if total is None else total + out
    return total.reshape(8, 16, 2 * LANES)


def halves(value):
    return jnp.where(
        lane_iota(16) < LANES // 2,
        pltpu.roll(value[:, :LANES], LANES - HALO, 1),
        pltpu.roll(value[:, LANES:], HALO, 1),
    )


def slots_of(tiles):
    return [(ref, index) for ref in tiles for index in range(ref.shape[0])]


def near_kernel(rows, xor, ntiles, taps_ref, radius_ref, labels, halo, *refs):
    tiles = slots_of(refs[:ntiles])
    bth, btl, acc, acc1, real_ref, base_ref, uh, ul, vh, vl = refs[ntiles:]
    where = Rows(rows, xor)
    blocks = [where.block(k) for k in range(len(tiles))]
    high, low, shift = tables(taps_ref, radius_ref)
    real_ref[...] = jnp.broadcast_to(shift, real_ref.shape)
    lines = [labels[j : j + 1, :] for j in range(len(tiles))]
    make_bands(where, blocks, high, low, lines, halo, base_ref, bth, btl)
    make_window(where, blocks, tiles, halo, uh, ul)
    acc[...] = jnp.zeros_like(acc)
    bands = lambda s, i: ((bth, btl)[i], s)
    where.each(lambda s: spread_rows(bands, uh, ul, 0, acc, s), len(tiles))
    if xor:
        blank = jnp.zeros((2, 16, 2 * LANES), BF16)
        for ref in (vh, vl):
            ref[0:2] = blank
        for ref, value in zip((vh, vl), split(acc[2:12] * where.inside()[None])):
            ref[2:12] = value
        for ref, value in zip((uh, ul), split(gather_rows(bands, vh, vl, 0))):
            ref[0:8] = value
        acc1[...] = jnp.zeros_like(acc1)
        spread_rows(bands, uh, ul, 0, acc1, 0)


def main_kernel(rows, xor, ndev, ntiles, taps_ref, radius_ref, real_ref, nbh, nbl, nacc, nacc1, *refs):
    if ntiles:
        labels, halo = refs[:2]
        tiles = slots_of(refs[2 : 2 + ntiles])
        refs = refs[2 + ntiles :]
    gram_ref, keep_ref, send_ref, uh, ul, fbh, fbl, base_ref, vh, vl, acc, kr, extra, copies, sems = refs
    where = Rows(rows, xor)
    pairs = rows * SUB // 2
    near = nbh.shape[0]
    shift = real_ref[0:1, :]
    shift = jnp.concatenate([shift, shift], 1)

    def bands(s, i):
        if xor and s >= near:
            return (fbh, fbl)[i], s - near
        return (nbh, nbl)[i], s

    blank = jnp.zeros((2, 16, 2 * LANES), BF16)
    for ref in (vh, vl):
        ref[0:2] = blank
        ref[pairs + 2 : pairs + 4] = blank
    inside = where.inside()

    acc[0 : near * 8 + 4] = nacc[...]
    if ntiles:
        acc[near * 8 + 4 :] = jnp.zeros((pairs - near * 8, 16, 2 * LANES), F32)
        blocks = [where.block(near + k) - near for k in range(len(tiles))]
        high, low, _ = tables(taps_ref, radius_ref)
        lines = [labels[j : j + 1, :] for j in range(ntiles)]
        make_bands(where, blocks, high, low, lines, halo, base_ref, fbh, fbl)
        make_window(where, blocks, tiles, halo, uh, ul)
        for s in range(near, rows):
            spread_rows(bands, uh, ul, near, acc, s)

    def finish(n, count):
        def body(s):
            start = s * 8
            value = acc[pl.ds(start + 2, 8)]
            if n > 0:
                value = value - shift * kr[n - 1, pl.ds(start, 8)]
            value = value * inside[None]
            kr[n, pl.ds(start, 8)] = value
            high, low = split(value)
            vh[pl.ds(start + 2, 8)] = high
            vl[pl.ds(start + 2, 8)] = low

        where.each(body, count)

    def forward(first, count, last):
        def body(s):
            total = gather_rows(bands, vh, vl, s)
            if last:
                kr[NB - 1, pl.ds(s * 8, 8)] = total
            for ref, value in zip((uh, ul), split(total)):
                ref[pl.ds(s * 8, 8)] = value

        where.each(body, count, first)

    fewer = rows - 1
    finish(0, rows)
    for n, first, into, out in ((1, 1, rows, rows), (2, 0, fewer, fewer)):
        forward(first, into, False)
        if n == 1 and xor:
            acc[0:12] = nacc1[...]
            acc[12:] = jnp.zeros((pairs - 8, 16, 2 * LANES), F32)
        else:
            acc[...] = jnp.zeros_like(acc)
        where.each(lambda s: spread_rows(bands, uh, ul, 0, acc, s), into, first)
        finish(n, out)
    forward(0, fewer, True)

    for side, (ref, row) in enumerate(zip((keep_ref, send_ref), where.own())):
        for n in range(NB):
            for p in range(8):
                value = halves(kr[n, row * 8 + p])
                if n < NB - 1:
                    ref[n, p] = value
                else:
                    extra[side, p] = value
    gram = jnp.zeros((NB * 16, NB * 16), F32)
    for p in range(8):
        stack = [
            jnp.concatenate([ref[n, p] for n in range(NB - 1)] + [extra[side, p]], 0)
            for side, ref in enumerate((keep_ref, send_ref))
        ]
        stack = jnp.concatenate(stack, 1)
        gram = gram + lax.dot_general(stack, stack, NT, precision=HIGHEST, preferred_element_type=F32)
    gram = jnp.concatenate([gram, jnp.zeros_like(gram)], 1)
    lanes, sub = lane_iota(16), lax.broadcasted_iota(jnp.int32, (16, LANES), 0)
    rel = lanes & 15

    def moved(i, j, a):
        return pltpu.roll(gram[16 * i : 16 * i + 16], (16 * (a - j)) % LANES, 1)

    message = jnp.zeros((16, LANES), F32)
    for a in range(NB - 1):
        even = moved(a, a, a)
        odd = moved(a, a + 1, a) if a < NB - 2 else moved(a + 1, a + 1, a) - shift[:, :LANES] * even
        here = lanes >> 4 == a
        message = jnp.where(here, jnp.where(sub >= rel, even, odd), message)
        corner = jnp.sum(jnp.where(here & (sub == rel), odd, 0.0), axis=1, keepdims=True)
        message = jnp.where(lanes == 48 + a, corner, message)
    message = jnp.where(lanes[:8] < LANES // 2, message[:8], pltpu.roll(message[8:], LANES // 2, 1))
    share = copies.shape[0]
    for dev in range(share):
        copies[dev] = message
    moves = [
        pltpu.make_async_copy(copies, gram_ref.at[pl.ds(i * share, share)], sems.at[i])
        for i in range(ndev // share)
    ]
    for move in moves:
        move.start()
    for move in moves:
        move.wait()


def last_kernel(rows, xor, real_ref, nbh, nbl, fbh, fbl, uh, ul, keep_ref, send_ref, keep3, send3, acc):
    where = Rows(rows, xor)
    near = nbh.shape[0]
    acc[...] = jnp.zeros_like(acc)
    bands = lambda s, i: ((nbh, nbl)[i], s)
    where.each(lambda s: spread_rows(bands, uh, ul, 0, acc, s), near)
    if xor:
        wh, wl = (stage_weights(ref, 0, True) for ref in (fbh, fbl))
        high = uh[near * 8 : near * 8 + 2].reshape(32, 2 * LANES)
        low = ul[near * 8 : near * 8 + 2].reshape(32, 2 * LANES)
        for t in (3, 4):
            out = product(high, low, wh[t], wl[t], NN).reshape(2, 16, 2 * LANES)
            acc[near * 8 + 4 - t : near * 8 + 6 - t] += out
    for ref, old, row in zip((keep3, send3), (keep_ref, send_ref), where.own()):
        for p in range(8):
            ref[p] = halves(acc[row * 8 + 2 + p]) - real_ref[0:1, :] * old[NB - 2, p]


def final_kernel(
    ndev, xor, real_ref, gram_ref, keep_ref, keep3, other_ref, other3, solution_ref, residual_ref
):
    r, q, _ = place()
    damp = real_ref[0:1, :] + 0.25 * DAMPING
    parts = [gram_ref[dev] for dev in range(ndev)]
    while len(parts) > 1:
        parts = [a + b for a, b in zip(parts[::2], parts[1::2])]
    lanes, sub = lane_iota(16), lax.broadcasted_iota(jnp.int32, (16, LANES), 0)
    shared = jnp.concatenate([parts[0], pltpu.roll(parts[0], LANES // 2, 1)], 0)
    turned = jnp.concatenate([shared] + [jnp.zeros_like(shared)] * 7, 0).T
    grams = []
    for a in range(NB - 1):
        block = pltpu.roll(shared, LANES - 16 * a, 1) if a else shared
        other = turned[16 * a : 16 * a + 16]
        corner = shared[:, 48 + a : 49 + a]
        grams.append(jnp.where(sub >= lanes, block, other))
        grams.append(jnp.where(sub < lanes, block, jnp.where(sub == lanes, corner, other)))

    def at(g, place):
        return pltpu.roll(grams[g], 16 * place, 1) if place else grams[g]

    lines = []
    for i in range(3):
        line = jnp.zeros((16, LANES), F32)
        for j in range(3):
            line = jnp.where(lanes >> 4 == j, at(i + j + 1, j) + damp * at(i + j, j), line)
        lines.append(jnp.where(lanes >> 4 == 3, at(i, 3), line))
    matrix = jnp.concatenate(lines, 0)
    index = lax.broadcasted_iota(jnp.int32, (48, LANES), 0)
    for panel in range(6):
        spread = [
            jnp.broadcast_to(matrix[:, 8 * panel + i : 8 * panel + i + 1], (48, LANES)) for i in range(8)
        ]
        for i in range(8):
            k = 8 * panel + i
            column = spread[i]
            inverse = 1.0 / column[k : k + 1, :]
            row = matrix[k : k + 1, :] * inverse
            scaled = column - (index == k).astype(F32)
            matrix = matrix - scaled * row
            for j in range(i + 1, 8):
                m = 8 * panel + j
                spread[j] = spread[j] - scaled * (column[m : m + 1, :] * inverse)
    c = [pltpu.roll(matrix[16 * i : 16 * i + 16], LANES - 48, 1) for i in range(3)]
    eye = (lax.broadcasted_iota(jnp.int32, (16, LANES), 0) == lanes).astype(F32)
    zero = jnp.zeros((16, LANES), F32)
    in_solution = [0.5 * c[0], 0.5 * c[1], 0.5 * c[2], zero]
    in_residual = [
        2.0 * (eye - damp * c[0]),
        -2.0 * (c[0] + damp * c[1]),
        -2.0 * (c[1] + damp * c[2]),
        -2.0 * c[2],
    ]
    weights = jnp.concatenate(
        [jnp.where(lanes < 16, a, pltpu.roll(b, 16, 1)) for a, b in zip(in_solution, in_residual)], 0
    )
    weights = jnp.concatenate([weights, jnp.zeros_like(weights)], 0).T[:32, : NB * 16]
    first = lanes < LANES // 2
    first2 = jnp.concatenate([first, first], 0)
    outs = (
        solution_ref.reshape(16 * SUB, LANES),
        residual_ref.reshape(16 * SUB, LANES),
    )
    for p in range(8):
        mine = jnp.concatenate([keep_ref[n, p] for n in range(NB - 1)] + [keep3[p]], 0)
        pair = jnp.concatenate([other_ref[n, p] for n in range(NB - 1)] + [other3[p]], 0)
        both = jnp.concatenate([mine, pair], 1)
        out = lax.dot_general(weights, both, NN, precision=HIGHEST, preferred_element_type=F32)
        a, b = out[:, :LANES], out[:, LANES:]
        left, right = jnp.where(q == 0, a, b), jnp.where(q == 0, b, a)
        even = jnp.where(first2, left, pltpu.roll(right, LANES // 2, 1))
        odd = jnp.where(first2, pltpu.roll(left, LANES // 2, 1), right)
        for i, line in ((2 * p, even), (2 * p + 1, odd)):
            i = i + (r >> 1) * (SUB - 1 - 2 * i) if xor else i
            for o, ref in enumerate(outs):
                ref[pl.ds(i, 16, stride=SUB), :] = line[16 * o : 16 * o + 16]


def per_device(measured, regions, kernels, radius):
    nrow, ncol = lax.axis_size("row"), lax.axis_size("col")
    ndev = nrow * ncol
    def flip(value, bit):
        return lax.ppermute(value, "row", [(i, i ^ bit) for i in range(nrow)])

    facing = []
    for i in range(nrow):
        for j in range(ncol):
            other = j + (1 if (i ^ j) & 1 else -1)
            if 0 <= other < ncol:
                facing.append((i * ncol + j, i * ncol + other))

    def call(kernel, name, out, operands, scratch, mib, specs=None):
        return pl.pallas_call(
            kernel,
            out_shape=[jax.ShapeDtypeStruct(shape, kind) for shape, kind in out],
            in_specs=[VMEM] * len(operands),
            out_specs=specs or [VMEM] * len(out),
            scratch_shapes=[pltpu.VMEM(*s) if isinstance(s, tuple) else s for s in scratch],
            compiler_params=params(mib),
            name=name,
        )(*operands)

    def bands_of(count):
        return ((count, K, LANES, LANES), BF16)

    def rows_of(count, kind):
        return ((count, 16, 2 * LANES), kind)

    def bases_of(count):
        return ((count, K, 8, LANES), F32)

    def edges_of(count):
        return ((count * (SUB // PACK), 16, LANES), F32)

    xor = nrow == 4
    if xor:
        mine = measured[None]
        tiles = [mine, flip(mine, 1)]
        labels = [regions, flip(regions, 1)]
        over = flip(mine, 2)
    else:
        tiles = [lax.all_gather(measured, "row", axis=0)]
        labels = [lax.all_gather(regions, "row", axis=0, tiled=True)]
    near, pairs = sum(t.shape[0] for t in tiles), nrow * SUB // 2
    edges, reach = call(
        first_kernel,
        "first",
        [edges_of(tiles[0].shape[0]), ((8, LANES), jnp.int32)],
        [tiles[0], radius[None]],
        [],
        4,
    )
    slots = edges_of(near)[0][0] + 1
    edges, tags = call(
        functools.partial(pack_kernel, len(labels)),
        "pack",
        [((slots, 16, LANES), F32), ((16, LANES), F32)],
        [edges, *labels, *tiles[1:]],
        [],
        4,
    )
    halo = lax.ppermute(edges, ("row", "col"), facing)
    taps = jnp.transpose(kernels, (1, 2, 0))
    nbh, nbl, nacc, nacc1, real = call(
        functools.partial(near_kernel, nrow, xor, len(tiles)),
        "near",
        [bands_of(near)] * 2 + [rows_of(near * 8 + 4, F32), rows_of(12, F32), ((8, LANES), F32)],
        [taps, reach, tags, halo, *tiles],
        [bases_of(near)] + [rows_of(near * 8, BF16)] * 2 + [rows_of(12, BF16)] * 2,
        8 + 2 * nrow,
    )
    far, ntiles = [], 0
    if xor:
        over, halo, tags = lax.optimization_barrier((over, halo, tags))
        far, ntiles = [flip(tags, 2), flip(halo, 2), over, flip(over, 1)], 2
    packed = ((NB - 1, 8, 16, LANES), F32)
    extra = max(nrow - near, 1)
    share = max(ndev // 8, 1)
    out = [((ndev, 8, LANES), F32), packed, packed] + [rows_of(pairs, BF16)] * 2 + [bands_of(extra)] * 2
    grams, keep, send, uh, ul, fbh, fbl = call(
        functools.partial(main_kernel, nrow, xor, ndev, ntiles),
        "krylov",
        out,
        [taps, reach, real, nbh, nbl, nacc, nacc1, *far],
        [bases_of(extra)]
        + [rows_of(pairs + 4, BF16)] * 2
        + [rows_of(pairs + 4, F32), ((NB, pairs, 16, 2 * LANES), F32), ((2, 8, 16, LANES), F32)]
        + [((share, 8, LANES), F32), pltpu.SemaphoreType.DMA((ndev // share,))],
        8 + 3 * nrow,
        [pl.BlockSpec(memory_space=pl.ANY)] + [VMEM] * (len(out) - 1),
    )
    grams = lax.all_to_all(grams, ("row", "col"), 0, 0)
    single = ((8, 16, LANES), F32)
    keep3, send3 = call(
        functools.partial(last_kernel, nrow, xor),
        "last",
        [single, single],
        [real, nbh, nbl, fbh, fbl, uh, ul, keep, send],
        [rows_of(near * 8 + 4, F32)],
        8 + 2 * nrow,
    )
    send, send3 = lax.optimization_barrier((send, send3))
    tile = ((16, SUB, LANES), F32)
    return tuple(
        call(
            functools.partial(final_kernel, ndev, xor),
            "combine",
            [tile, tile],
            [real, grams, keep, keep3, flip(send, 1), flip(send3, 1)],
            [],
            8,
        )
    )


def solution(mesh):
    in_specs = (P(None, "row", "col"), P("row", "col"), P(), P())
    out_specs = (P(None, "row", "col"), P(None, "row", "col"))
    return jax.shard_map(
        per_device, mesh=mesh, in_specs=in_specs, out_specs=out_specs, check_vma=False
    )
```

```python
import functools

import jax
import jax.numpy as jnp
from jax import lax
from jax.experimental import pallas as pl
from jax.experimental.pallas import tpu as pltpu
from jax.sharding import PartitionSpec as P

R = 4
K = 9
SUB = 16
REG = 64
DAMPING = 0.1

LANES = 128
HALO = 32
PACK = LANES // HALO
NB = 4

F32 = jnp.float32
BF16 = jnp.bfloat16
NN = (((1,), (0,)), ((), ()))
NT = (((1,), (1,)), ((), ()))
VMEM = pl.BlockSpec(memory_space=pltpu.VMEM)
SMEM = pl.BlockSpec(memory_space=pltpu.SMEM)
def params(mib):
    return pltpu.CompilerParams(vmem_limit_bytes=mib << 20)


def split(value):
    high = value.astype(BF16)
    return high, (value - high.astype(F32)).astype(BF16)


def lane_iota(rows):
    return lax.broadcasted_iota(jnp.int32, (rows, LANES), 1)


def row_of(ref, index, row):
    frames, rows = ref.shape[1], ref.shape[2]
    flat = ref.reshape(ref.shape[0] * frames * rows, LANES)
    return flat[pl.ds(index * frames * rows + row, frames, stride=rows), :]


def place():
    r, c = lax.axis_index("row"), lax.axis_index("col")
    q = (r ^ c) & 1
    beside = jnp.where(q == 0, c > 0, c < lax.axis_size("col") - 1)
    return r, q, beside.astype(jnp.int32)


def pack_tile(tile, index, out, slot):
    q = place()[1]
    for group in range(SUB // PACK):
        packed = None
        for m in range(PACK):
            line = row_of(tile, index, group * PACK + m)
            line = pltpu.roll(line, HALO * m + HALO * q, 1)
            lanes = lane_iota(line.shape[0])
            packed = line if packed is None else jnp.where(lanes >= HALO * m, line, packed)
        out[slot + group] = packed


def first_kernel(tile, radius_ref, out, reach_ref):
    for index in range(tile.shape[0]):
        pack_tile(tile, index, out, index * (SUB // PACK))
    reach_ref[...] = jnp.zeros_like(reach_ref)
    reach_ref[0:1, :REG] = radius_ref[...]


def pack_kernel(nlabels, packed, *refs):
    labels, tiles, (out, tags) = refs[:nlabels], refs[nlabels:-2], refs[-2:]
    slot = packed.shape[0]
    out[:slot] = packed[...]
    for tile in tiles:
        pack_tile(tile, 0, out, slot)
        slot += SUB // PACK
    tags[...] = jnp.zeros((16, LANES), F32)
    line = 0
    for ref in labels:
        height, width = ref.shape
        tags[line : line + height, :width] = (ref[...] + 1).astype(F32)
        line += height
    out[slot] = tags[...]


def stage_weights(bt, s, transposed):
    zero = jnp.zeros((LANES, LANES), BF16)

    def block(a):
        return bt[s, a] if 0 <= a < K else zero

    blocks = []
    for t in range(5):
        if transposed:
            index = [[2 * t + i - o for o in range(2)] for i in range(2)]
        else:
            index = [[8 - 2 * t + o - i for i in range(2)] for o in range(2)]
        blocks.append(
            jnp.concatenate([jnp.concatenate([block(a) for a in line], 1) for line in index], 0)
        )
    return blocks


class Rows:
    def __init__(self, rows, xor):
        self.rows, self.xor = rows, xor
        self.r, self.q, self.beside = place()
        self.down = (self.r >> 1) if xor else 0
        lanes = lane_iota(16)
        start = (LANES - HALO) * self.q
        self.in_halo = (lanes >= start) & (lanes < start + HALO)

    def block(self, k):
        return (k & 2) + ((k ^ self.r ^ self.down) & 1) if self.xor else k

    def turn(self, i, last):
        return i + self.down * (last - 2 * i) if self.xor else i

    def each(self, body, count, first=0):
        if self.xor:
            for s in range(first, count):
                body(s)
        else:
            lax.fori_loop(0, self.rows, lambda s, c: (body(s), c)[1], 0)

    def inside(self):
        mask = jnp.where(self.in_halo, self.beside.astype(F32), 1.0)
        return jnp.concatenate([mask, mask], 1)

    def own(self):
        return (self.block(0), self.block(1)) if self.xor else (self.r, self.r ^ 1)


def tables(taps_ref, radius_ref):
    radius = radius_ref[0:1, :REG]
    high, low, total = [], [], jnp.zeros((1, REG), F32)
    b = lax.broadcasted_iota(jnp.int32, (K, REG), 0)
    for a in range(K):
        reach = jnp.maximum(jnp.abs(b - R), abs(a - R))
        taps = jnp.where(reach <= radius, 0.5 * taps_ref[a], 0.0)
        total = total + jnp.sum(taps, axis=0, keepdims=True)
        for part, value in zip((high, low), split(taps)):
            part.append(value)
    squares = total * total
    mean = jnp.sum(squares, axis=1, keepdims=True) * (1.0 / REG)
    return high, low, 0.5 * jnp.sqrt(mean * jnp.max(squares, axis=1, keepdims=True))


def make_bands(where, blocks, high, low, labels, halo, base_ref, bth, btl):
    lanes = lane_iota(8)
    count = len(blocks)
    hots = []
    for j in range(count):
        own = jnp.broadcast_to(labels[j], (8, LANES))
        beside = jnp.broadcast_to(halo[count * (SUB // PACK) + j // 16, j % 16 : j % 16 + 1, :], (8, LANES))
        left = jnp.where(lanes < 2, pltpu.roll(beside, LANES - 6, 1), pltpu.roll(own, 2, 1))
        right = jnp.where(lanes < 6, pltpu.roll(own, LANES - 2, 1), pltpu.roll(beside, 6, 1))
        window = jnp.where(where.q == 0, left, right)
        diagonal = lanes == lax.broadcasted_iota(jnp.int32, (8, LANES), 0)
        column = jnp.sum(jnp.where(diagonal, window, 0.0), axis=1, keepdims=True)
        hots.append((column == (lanes[:, :REG] + 1).astype(F32)).astype(F32))
    hot = jnp.concatenate(hots, 0).astype(BF16)
    b = lax.broadcasted_iota(jnp.int32, (K, LANES), 0)
    spread = (lax.broadcasted_iota(jnp.int32, (K, LANES), 1) == (LANES + R - b) % LANES).astype(BF16)
    for a in range(K):
        base = None
        for part in (high, low):
            picked = lax.dot_general(hot, part[a], NT, preferred_element_type=F32).astype(BF16)
            line = lax.dot_general(picked, spread, NN, preferred_element_type=F32)
            base = line if base is None else base + line
        for j in range(count):
            base_ref[j, a] = base[8 * j : 8 * j + 8]
    for j, s in enumerate(blocks):
        for a in range(K):
            squares = base_ref[j, where.turn(a, K - 1)]
            for c in range(LANES // SUB):
                band = jnp.broadcast_to(squares[c : c + 1], (SUB, LANES))
                band = pltpu.roll(band, SUB * c, 1, stride=1, stride_axis=0)
                for ref, value in zip((bth, btl), split(band)):
                    ref[s, a, c * SUB : (c + 1) * SUB, :] = value


def make_window(where, blocks, tiles, halo, uh, ul):
    for j, (s, (ref, index)) in enumerate(zip(blocks, tiles)):
        for p in range(SUB // 2):
            parts = []
            for row in (2 * p, 2 * p + 1):
                i = where.turn(row, SUB - 1)
                line = row_of(ref, index, row)
                if where.xor:
                    line = jnp.where(where.down > 0, row_of(ref, index, SUB - 1 - row), line)
                line = pltpu.roll(line, HALO + (LANES - 2 * HALO) * where.q, 1)
                edge = halo[j * (SUB // PACK) + i // PACK]
                edge = pltpu.roll(edge, (LANES - HALO * (i % PACK) + (LANES - HALO) * where.q) % LANES, 1)
                parts.append(jnp.where(where.in_halo, edge, line))
            for out, value in zip((uh, ul), split(jnp.concatenate(parts, 1))):
                out[s * (SUB // 2) + p] = value


def product(high, low, wh, wl, dims):
    both = lax.dot_general(jnp.concatenate([high, low], 0), wh, dims, preferred_element_type=F32)
    third = lax.dot_general(high, wl, dims, preferred_element_type=F32)
    return both[: high.shape[0]] + both[high.shape[0] :] + third


def three(value):
    parts = []
    for _ in range(3):
        parts.append(value.astype(BF16))
        value = value - parts[-1].astype(F32)
    return parts


def exact_gram(value):
    parts = jnp.concatenate(three(value), 0)
    out = lax.dot_general(parts, parts, NT, preferred_element_type=F32)
    rows = value.shape[0]
    blocks = [[out[rows * i : rows * i + rows, rows * j : rows * j + rows] for j in range(3)] for i in range(3)]
    small = (blocks[1][1] + (blocks[0][2] + blocks[2][0])) + (blocks[1][2] + blocks[2][1])
    return blocks[0][0] + ((blocks[0][1] + blocks[1][0]) + small)


def exact_weights(weights):
    high, mid, low = three(weights)
    zero = jnp.zeros_like(high)
    lines = ([high] * 3, [mid, mid, zero], [low, zero, zero])
    return jnp.concatenate([jnp.concatenate(line, 1) for line in lines], 0)


def exact_combination(weights, value):
    out = lax.dot_general(weights, jnp.concatenate(three(value), 0), NN, preferred_element_type=F32)
    rows = weights.shape[0] // 3
    return out[:rows] + (out[rows : 2 * rows] + out[2 * rows :])


def spread_rows(bands, uh, ul, base, acc, s):
    wh, wl = (stage_weights(*bands(s, i), True) for i in range(2))
    start = (s - base) * 8
    high = uh[pl.ds(start, 8)].reshape(128, 2 * LANES)
    low = ul[pl.ds(start, 8)].reshape(128, 2 * LANES)
    for t in range(5):
        out = product(high, low, wh[t], wl[t], NN).reshape(8, 16, 2 * LANES)
        acc[pl.ds(s * 8 + 4 - t, 8)] += out


def gather_rows(bands, vh, vl, s):
    wh, wl = (stage_weights(*bands(s, i), False) for i in range(2))
    total = None
    for t in range(5):
        high = vh[pl.ds(s * 8 + t, 8)].reshape(128, 2 * LANES)
        low = vl[pl.ds(s * 8 + t, 8)].reshape(128, 2 * LANES)
        out = product(high, low, wh[t], wl[t], NT)
        total = out if total is None else total + out
    return total.reshape(8, 16, 2 * LANES)


def halves(value):
    return jnp.where(
        lane_iota(16) < LANES // 2,
        pltpu.roll(value[:, :LANES], LANES - HALO, 1),
        pltpu.roll(value[:, LANES:], HALO, 1),
    )


def slots_of(tiles):
    return [(ref, index) for ref in tiles for index in range(ref.shape[0])]


def near_kernel(rows, xor, ntiles, taps_ref, radius_ref, labels, halo, *refs):
    tiles = slots_of(refs[:ntiles])
    bth, btl, acc, acc1, real_ref, base_ref, uh, ul, vh, vl = refs[ntiles:]
    where = Rows(rows, xor)
    blocks = [where.block(k) for k in range(len(tiles))]
    high, low, shift = tables(taps_ref, radius_ref)
    real_ref[...] = jnp.broadcast_to(shift, real_ref.shape)
    lines = [labels[j : j + 1, :] for j in range(len(tiles))]
    make_bands(where, blocks, high, low, lines, halo, base_ref, bth, btl)
    make_window(where, blocks, tiles, halo, uh, ul)
    acc[...] = jnp.zeros_like(acc)
    bands = lambda s, i: ((bth, btl)[i], s)
    where.each(lambda s: spread_rows(bands, uh, ul, 0, acc, s), len(tiles))
    if xor:
        blank = jnp.zeros((2, 16, 2 * LANES), BF16)
        for ref in (vh, vl):
            ref[0:2] = blank
        for ref, value in zip((vh, vl), split(acc[2:12] * where.inside()[None])):
            ref[2:12] = value
        for ref, value in zip((uh, ul), split(gather_rows(bands, vh, vl, 0))):
            ref[0:8] = value
        acc1[...] = jnp.zeros_like(acc1)
        spread_rows(bands, uh, ul, 0, acc1, 0)


def main_kernel(rows, xor, ndev, ntiles, taps_ref, radius_ref, real_ref, nbh, nbl, nacc, nacc1, *refs):
    if ntiles:
        labels, halo = refs[:2]
        tiles = slots_of(refs[2 : 2 + ntiles])
        refs = refs[2 + ntiles :]
    gram_ref, keep_ref, send_ref, uh, ul, fbh, fbl, base_ref, vh, vl, acc, kr, extra, copies, sems = refs
    where = Rows(rows, xor)
    pairs = rows * SUB // 2
    near = nbh.shape[0]
    shift = real_ref[0:1, :]
    shift = jnp.concatenate([shift, shift], 1)

    def bands(s, i):
        if xor and s >= near:
            return (fbh, fbl)[i], s - near
        return (nbh, nbl)[i], s

    blank = jnp.zeros((2, 16, 2 * LANES), BF16)
    for ref in (vh, vl):
        ref[0:2] = blank
        ref[pairs + 2 : pairs + 4] = blank
    inside = where.inside()

    acc[0 : near * 8 + 4] = nacc[...]
    if ntiles:
        acc[near * 8 + 4 :] = jnp.zeros((pairs - near * 8, 16, 2 * LANES), F32)
        blocks = [where.block(near + k) - near for k in range(len(tiles))]
        high, low, _ = tables(taps_ref, radius_ref)
        lines = [labels[j : j + 1, :] for j in range(ntiles)]
        make_bands(where, blocks, high, low, lines, halo, base_ref, fbh, fbl)
        make_window(where, blocks, tiles, halo, uh, ul)
        for s in range(near, rows):
            spread_rows(bands, uh, ul, near, acc, s)

    def finish(n, count):
        def body(s):
            start = s * 8
            value = acc[pl.ds(start + 2, 8)]
            if n > 0:
                value = value - shift * kr[n - 1, pl.ds(start, 8)]
            value = value * inside[None]
            kr[n, pl.ds(start, 8)] = value
            high, low = split(value)
            vh[pl.ds(start + 2, 8)] = high
            vl[pl.ds(start + 2, 8)] = low

        where.each(body, count)

    def forward(first, count, last):
        def body(s):
            total = gather_rows(bands, vh, vl, s)
            if last:
                kr[NB - 1, pl.ds(s * 8, 8)] = total
            for ref, value in zip((uh, ul), split(total)):
                ref[pl.ds(s * 8, 8)] = value

        where.each(body, count, first)

    fewer = rows - 1
    finish(0, rows)
    for n, first, into, out in ((1, 1, rows, rows), (2, 0, fewer, fewer)):
        forward(first, into, False)
        if n == 1 and xor:
            acc[0:12] = nacc1[...]
            acc[12:] = jnp.zeros((pairs - 8, 16, 2 * LANES), F32)
        else:
            acc[...] = jnp.zeros_like(acc)
        where.each(lambda s: spread_rows(bands, uh, ul, 0, acc, s), into, first)
        finish(n, out)
    forward(0, fewer, True)

    for side, (ref, row) in enumerate(zip((keep_ref, send_ref), where.own())):
        for n in range(NB):
            for p in range(8):
                value = halves(kr[n, row * 8 + p])
                if n < NB - 1:
                    ref[n, p] = value
                else:
                    extra[side, p] = value
    gram = jnp.zeros((NB * 16, NB * 16), F32)
    for p in range(8):
        stack = [
            jnp.concatenate([ref[n, p] for n in range(NB - 1)] + [extra[side, p]], 0)
            for side, ref in enumerate((keep_ref, send_ref))
        ]
        stack = jnp.concatenate(stack, 1)
        gram = gram + exact_gram(stack)
    gram = jnp.concatenate([gram, jnp.zeros_like(gram)], 1)
    lanes, sub = lane_iota(16), lax.broadcasted_iota(jnp.int32, (16, LANES), 0)
    rel = lanes & 15

    def moved(i, j, a):
        return pltpu.roll(gram[16 * i : 16 * i + 16], (16 * (a - j)) % LANES, 1)

    message = jnp.zeros((16, LANES), F32)
    for a in range(NB - 1):
        even = moved(a, a, a)
        odd = moved(a, a + 1, a) if a < NB - 2 else moved(a + 1, a + 1, a) - shift[:, :LANES] * even
        here = lanes >> 4 == a
        message = jnp.where(here, jnp.where(sub >= rel, even, odd), message)
        corner = jnp.sum(jnp.where(here & (sub == rel), odd, 0.0), axis=1, keepdims=True)
        message = jnp.where(lanes == 48 + a, corner, message)
    message = jnp.where(lanes[:8] < LANES // 2, message[:8], pltpu.roll(message[8:], LANES // 2, 1))
    share = copies.shape[0]
    for dev in range(share):
        copies[dev] = message
    moves = [
        pltpu.make_async_copy(copies, gram_ref.at[pl.ds(i * share, share)], sems.at[i])
        for i in range(ndev // share)
    ]
    for move in moves:
        move.start()
    for move in moves:
        move.wait()


def last_kernel(rows, xor, real_ref, nbh, nbl, fbh, fbl, uh, ul, keep_ref, send_ref, keep3, send3, acc):
    where = Rows(rows, xor)
    near = nbh.shape[0]
    acc[...] = jnp.zeros_like(acc)
    bands = lambda s, i: ((nbh, nbl)[i], s)
    where.each(lambda s: spread_rows(bands, uh, ul, 0, acc, s), near)
    if xor:
        wh, wl = (stage_weights(ref, 0, True) for ref in (fbh, fbl))
        high = uh[near * 8 : near * 8 + 2].reshape(32, 2 * LANES)
        low = ul[near * 8 : near * 8 + 2].reshape(32, 2 * LANES)
        for t in (3, 4):
            out = product(high, low, wh[t], wl[t], NN).reshape(2, 16, 2 * LANES)
            acc[near * 8 + 4 - t : near * 8 + 6 - t] += out
    for ref, old, row in zip((keep3, send3), (keep_ref, send_ref), where.own()):
        for p in range(8):
            ref[p] = halves(acc[row * 8 + 2 + p]) - real_ref[0:1, :] * old[NB - 2, p]


def final_kernel(
    ndev, xor, real_ref, gram_ref, keep_ref, keep3, other_ref, other3, solution_ref, residual_ref
):
    r, q, _ = place()
    damp = real_ref[0:1, :] + 0.25 * DAMPING
    parts = [gram_ref[dev] for dev in range(ndev)]
    while len(parts) > 1:
        parts = [a + b for a, b in zip(parts[::2], parts[1::2])]
    lanes, sub = lane_iota(16), lax.broadcasted_iota(jnp.int32, (16, LANES), 0)
    shared = jnp.concatenate([parts[0], pltpu.roll(parts[0], LANES // 2, 1)], 0)
    turned = jnp.concatenate([shared] + [jnp.zeros_like(shared)] * 7, 0).T
    grams = []
    for a in range(NB - 1):
        block = pltpu.roll(shared, LANES - 16 * a, 1) if a else shared
        other = turned[16 * a : 16 * a + 16]
        corner = shared[:, 48 + a : 49 + a]
        grams.append(jnp.where(sub >= lanes, block, other))
        grams.append(jnp.where(sub < lanes, block, jnp.where(sub == lanes, corner, other)))

    def at(g, place):
        return pltpu.roll(grams[g], 16 * place, 1) if place else grams[g]

    def line_of(entry):
        line = jnp.zeros((16, LANES), F32)
        for j in range(3):
            line = jnp.where(lanes >> 4 == j, entry(j), line)
        return line

    lines = [line_of(lambda j: at(i + j + 1, j) + damp * at(i + j, j)) for i in range(3)]
    matrix = jnp.concatenate(lines + [line_of(lambda j: at(j, j))], 0)
    lane = lane_iota(1)
    for panel in range(6):
        spread = [
            jnp.broadcast_to(matrix[:, 8 * panel + i : 8 * panel + i + 1], (64, LANES)) for i in range(8)
        ]
        for i in range(8):
            k = 8 * panel + i
            column = spread[i]
            scaled = column * (1.0 / column[k : k + 1, :])
            matrix = matrix - scaled * (matrix[k : k + 1, :] - (lane == k).astype(F32))
            for j in range(i + 1, 8):
                m = 8 * panel + j
                spread[j] = spread[j] - scaled * column[m : m + 1, :]
    c = jnp.where(lanes < 48, matrix[48:], 0.0)
    eye = (sub == lanes).astype(F32)
    weights = jnp.concatenate([0.5 * c, 2.0 * (eye - damp * c - pltpu.roll(c, 16, 1))], 0)[:, : NB * 16]
    weights = exact_weights(weights)
    down = r >> 1
    first = lanes < LANES // 2
    first2 = jnp.concatenate([first, first], 0)
    outs = (
        solution_ref.reshape(16 * SUB, LANES),
        residual_ref.reshape(16 * SUB, LANES),
    )
    for p in range(8):
        at = p + down * (7 - 2 * p) if xor else p
        mine = jnp.concatenate([keep_ref[n, at] for n in range(NB - 1)] + [keep3[at]], 0)
        pair = jnp.concatenate([other_ref[n, at] for n in range(NB - 1)] + [other3[at]], 0)
        both = jnp.concatenate([mine, pair], 1)
        out = exact_combination(weights, both)
        a, b = out[:, :LANES], out[:, LANES:]
        left, right = jnp.where(q == 0, a, b), jnp.where(q == 0, b, a)
        even = jnp.where(first2, left, pltpu.roll(right, LANES // 2, 1))
        odd = jnp.where(first2, pltpu.roll(left, LANES // 2, 1), right)
        if xor:
            even, odd = jnp.where(down > 0, odd, even), jnp.where(down > 0, even, odd)
        for i, line in ((2 * p, even), (2 * p + 1, odd)):
            for o, ref in enumerate(outs):
                ref[pl.ds(i, 16, stride=SUB), :] = line[16 * o : 16 * o + 16]


def per_device(measured, regions, kernels, radius):
    nrow, ncol = lax.axis_size("row"), lax.axis_size("col")
    ndev = nrow * ncol
    def flip(value, bit):
        return lax.ppermute(value, "row", [(i, i ^ bit) for i in range(nrow)])

    facing = []
    for i in range(nrow):
        for j in range(ncol):
            other = j + (1 if (i ^ j) & 1 else -1)
            if 0 <= other < ncol:
                facing.append((i * ncol + j, i * ncol + other))

    def call(kernel, name, out, operands, scratch, mib, specs=None):
        return pl.pallas_call(
            kernel,
            out_shape=[jax.ShapeDtypeStruct(shape, kind) for shape, kind in out],
            in_specs=[VMEM] * len(operands),
            out_specs=specs or [VMEM] * len(out),
            scratch_shapes=[pltpu.VMEM(*s) if isinstance(s, tuple) else s for s in scratch],
            compiler_params=params(mib),
            name=name,
        )(*operands)

    def bands_of(count):
        return ((count, K, LANES, LANES), BF16)

    def rows_of(count, kind):
        return ((count, 16, 2 * LANES), kind)

    def bases_of(count):
        return ((count, K, 8, LANES), F32)

    def edges_of(count):
        return ((count * (SUB // PACK), 16, LANES), F32)

    xor = nrow == 4
    if xor:
        mine = measured[None]
        tiles = [mine, flip(mine, 1)]
        labels = [regions, flip(regions, 1)]
        over = flip(mine, 2)
    else:
        tiles = [lax.all_gather(measured, "row", axis=0)]
        labels = [lax.all_gather(regions, "row", axis=0, tiled=True)]
    near, pairs = sum(t.shape[0] for t in tiles), nrow * SUB // 2
    edges, reach = call(
        first_kernel,
        "first",
        [edges_of(tiles[0].shape[0]), ((8, LANES), jnp.int32)],
        [tiles[0], radius[None]],
        [],
        4,
    )
    slots = edges_of(near)[0][0] + 1
    edges, tags = call(
        functools.partial(pack_kernel, len(labels)),
        "pack",
        [((slots, 16, LANES), F32), ((16, LANES), F32)],
        [edges, *labels, *tiles[1:]],
        [],
        4,
    )
    halo = lax.ppermute(edges, ("row", "col"), facing)
    taps = jnp.transpose(kernels, (1, 2, 0))
    nbh, nbl, nacc, nacc1, real = call(
        functools.partial(near_kernel, nrow, xor, len(tiles)),
        "near",
        [bands_of(near)] * 2 + [rows_of(near * 8 + 4, F32), rows_of(12, F32), ((8, LANES), F32)],
        [taps, reach, tags, halo, *tiles],
        [bases_of(near)] + [rows_of(near * 8, BF16)] * 2 + [rows_of(12, BF16)] * 2,
        8 + 2 * nrow,
    )
    far, ntiles = [], 0
    if xor:
        over, halo, tags = lax.optimization_barrier((over, halo, tags))
        far, ntiles = [flip(tags, 2), flip(halo, 2), over, flip(over, 1)], 2
    packed = ((NB - 1, 8, 16, LANES), F32)
    extra = max(nrow - near, 1)
    share = max(ndev // 8, 1)
    out = [((ndev, 8, LANES), F32), packed, packed] + [rows_of(pairs, BF16)] * 2 + [bands_of(extra)] * 2
    grams, keep, send, uh, ul, fbh, fbl = call(
        functools.partial(main_kernel, nrow, xor, ndev, ntiles),
        "krylov",
        out,
        [taps, reach, real, nbh, nbl, nacc, nacc1, *far],
        [bases_of(extra)]
        + [rows_of(pairs + 4, BF16)] * 2
        + [rows_of(pairs + 4, F32), ((NB, pairs, 16, 2 * LANES), F32), ((2, 8, 16, LANES), F32)]
        + [((share, 8, LANES), F32), pltpu.SemaphoreType.DMA((ndev // share,))],
        8 + 3 * nrow,
        [pl.BlockSpec(memory_space=pl.ANY)] + [VMEM] * (len(out) - 1),
    )
    grams = lax.all_to_all(grams, ("row", "col"), 0, 0)
    single = ((8, 16, LANES), F32)
    keep3, send3 = call(
        functools.partial(last_kernel, nrow, xor),
        "last",
        [single, single],
        [real, nbh, nbl, fbh, fbl, uh, ul, keep, send],
        [rows_of(near * 8 + 4, F32)],
        8 + 2 * nrow,
    )
    send, send3 = lax.optimization_barrier((send, send3))
    tile = ((16, SUB, LANES), F32)
    return tuple(
        call(
            functools.partial(final_kernel, ndev, xor),
            "combine",
            [tile, tile],
            [real, grams, keep, keep3, flip(send, 1), flip(send3, 1)],
            [],
            8,
        )
    )


def solution(mesh):
    in_specs = (P(None, "row", "col"), P("row", "col"), P(), P())
    out_specs = (P(None, "row", "col"), P(None, "row", "col"))
    return jax.shard_map(
        per_device, mesh=mesh, in_specs=in_specs, out_specs=out_specs, check_vma=False
    )
```

```python
import functools

import jax
import jax.numpy as jnp
from jax import lax
from jax.experimental import pallas as pl
from jax.experimental.pallas import tpu as pltpu
from jax.sharding import PartitionSpec as P

R = 4
K = 9
SUB = 16
REG = 64
DAMPING = 0.1

LANES = 128
HALO = 32
PACK = LANES // HALO
NB = 4

F32 = jnp.float32
BF16 = jnp.bfloat16
NN = (((1,), (0,)), ((), ()))
NT = (((1,), (1,)), ((), ()))
VMEM = pl.BlockSpec(memory_space=pltpu.VMEM)
SMEM = pl.BlockSpec(memory_space=pltpu.SMEM)
def params(mib):
    return pltpu.CompilerParams(vmem_limit_bytes=mib << 20)


def split(value):
    high = value.astype(BF16)
    return high, (value - high.astype(F32)).astype(BF16)


def lane_iota(rows):
    return lax.broadcasted_iota(jnp.int32, (rows, LANES), 1)


def row_of(ref, index, row):
    frames, rows = ref.shape[1], ref.shape[2]
    flat = ref.reshape(ref.shape[0] * frames * rows, LANES)
    return flat[pl.ds(index * frames * rows + row, frames, stride=rows), :]


def place():
    r, c = lax.axis_index("row"), lax.axis_index("col")
    q = (r ^ c) & 1
    beside = jnp.where(q == 0, c > 0, c < lax.axis_size("col") - 1)
    return r, q, beside.astype(jnp.int32)


def pack_tile(tile, index, out, slot):
    q = place()[1]
    for group in range(SUB // PACK):
        packed = None
        for m in range(PACK):
            line = row_of(tile, index, group * PACK + m)
            line = pltpu.roll(line, HALO * m + HALO * q, 1)
            lanes = lane_iota(line.shape[0])
            packed = line if packed is None else jnp.where(lanes >= HALO * m, line, packed)
        out[slot + group] = packed


def first_kernel(tile, radius_ref, out, reach_ref):
    for index in range(tile.shape[0]):
        pack_tile(tile, index, out, index * (SUB // PACK))
    reach_ref[...] = jnp.zeros_like(reach_ref)
    reach_ref[0:1, :REG] = radius_ref[...]


def pack_kernel(nlabels, packed, *refs):
    labels, tiles, (out, tags) = refs[:nlabels], refs[nlabels:-2], refs[-2:]
    slot = packed.shape[0]
    out[:slot] = packed[...]
    for tile in tiles:
        pack_tile(tile, 0, out, slot)
        slot += SUB // PACK
    tags[...] = jnp.zeros((16, LANES), F32)
    line = 0
    for ref in labels:
        height, width = ref.shape
        tags[line : line + height, :width] = (ref[...] + 1).astype(F32)
        line += height
    out[slot] = tags[...]


def stage_weights(bt, s, transposed):
    zero = jnp.zeros((LANES, LANES), BF16)

    def block(a):
        return bt[s, a] if 0 <= a < K else zero

    blocks = []
    for t in range(5):
        if transposed:
            index = [[2 * t + i - o for o in range(2)] for i in range(2)]
        else:
            index = [[8 - 2 * t + o - i for i in range(2)] for o in range(2)]
        blocks.append(
            jnp.concatenate([jnp.concatenate([block(a) for a in line], 1) for line in index], 0)
        )
    return blocks


class Rows:
    def __init__(self, rows, xor):
        self.rows, self.xor = rows, xor
        self.r, self.q, self.beside = place()
        self.down = (self.r >> 1) if xor else 0
        lanes = lane_iota(16)
        start = (LANES - HALO) * self.q
        self.in_halo = (lanes >= start) & (lanes < start + HALO)

    def block(self, k):
        return (k & 2) + ((k ^ self.r ^ self.down) & 1) if self.xor else k

    def turn(self, i, last):
        return i + self.down * (last - 2 * i) if self.xor else i

    def each(self, body, count, first=0):
        if self.xor:
            for s in range(first, count):
                body(s)
        else:
            lax.fori_loop(0, self.rows, lambda s, c: (body(s), c)[1], 0)

    def inside(self):
        mask = jnp.where(self.in_halo, self.beside.astype(F32), 1.0)
        return jnp.concatenate([mask, mask], 1)

    def own(self):
        return (self.block(0), self.block(1)) if self.xor else (self.r, self.r ^ 1)


def tables(taps_ref, radius_ref):
    radius = radius_ref[0:1, :REG]
    high, low, total = [], [], jnp.zeros((1, REG), F32)
    b = lax.broadcasted_iota(jnp.int32, (K, REG), 0)
    for a in range(K):
        reach = jnp.maximum(jnp.abs(b - R), abs(a - R))
        taps = jnp.where(reach <= radius, 0.5 * taps_ref[a], 0.0)
        total = total + jnp.sum(taps, axis=0, keepdims=True)
        for part, value in zip((high, low), split(taps)):
            part.append(value)
    squares = total * total
    mean = jnp.sum(squares, axis=1, keepdims=True) * (1.0 / REG)
    return high, low, 0.5 * jnp.sqrt(mean * jnp.max(squares, axis=1, keepdims=True))


def make_bands(where, blocks, high, low, labels, halo, base_ref, bth, btl):
    lanes = lane_iota(8)
    count = len(blocks)
    hots = []
    for j in range(count):
        own = jnp.broadcast_to(labels[j], (8, LANES))
        beside = jnp.broadcast_to(halo[count * (SUB // PACK) + j // 16, j % 16 : j % 16 + 1, :], (8, LANES))
        left = jnp.where(lanes < 2, pltpu.roll(beside, LANES - 6, 1), pltpu.roll(own, 2, 1))
        right = jnp.where(lanes < 6, pltpu.roll(own, LANES - 2, 1), pltpu.roll(beside, 6, 1))
        window = jnp.where(where.q == 0, left, right)
        diagonal = lanes == lax.broadcasted_iota(jnp.int32, (8, LANES), 0)
        column = jnp.sum(jnp.where(diagonal, window, 0.0), axis=1, keepdims=True)
        hots.append((column == (lanes[:, :REG] + 1).astype(F32)).astype(F32))
    hot = jnp.concatenate(hots, 0).astype(BF16)
    b = lax.broadcasted_iota(jnp.int32, (K, LANES), 0)
    spread = (lax.broadcasted_iota(jnp.int32, (K, LANES), 1) == (LANES + R - b) % LANES).astype(BF16)
    for a in range(K):
        base = None
        for part in (high, low):
            picked = lax.dot_general(hot, part[a], NT, preferred_element_type=F32).astype(BF16)
            line = lax.dot_general(picked, spread, NN, preferred_element_type=F32)
            base = line if base is None else base + line
        for j in range(count):
            base_ref[j, a] = base[8 * j : 8 * j + 8]
    for j, s in enumerate(blocks):
        for a in range(K):
            squares = base_ref[j, where.turn(a, K - 1)]
            for c in range(LANES // SUB):
                band = jnp.broadcast_to(squares[c : c + 1], (SUB, LANES))
                band = pltpu.roll(band, SUB * c, 1, stride=1, stride_axis=0)
                for ref, value in zip((bth, btl), split(band)):
                    ref[s, a, c * SUB : (c + 1) * SUB, :] = value


def make_window(where, blocks, tiles, halo, uh, ul):
    for j, (s, (ref, index)) in enumerate(zip(blocks, tiles)):
        for p in range(SUB // 2):
            parts = []
            for row in (2 * p, 2 * p + 1):
                i = where.turn(row, SUB - 1)
                line = row_of(ref, index, row)
                if where.xor:
                    line = jnp.where(where.down > 0, row_of(ref, index, SUB - 1 - row), line)
                line = pltpu.roll(line, HALO + (LANES - 2 * HALO) * where.q, 1)
                edge = halo[j * (SUB // PACK) + i // PACK]
                edge = pltpu.roll(edge, (LANES - HALO * (i % PACK) + (LANES - HALO) * where.q) % LANES, 1)
                parts.append(jnp.where(where.in_halo, edge, line))
            for out, value in zip((uh, ul), split(jnp.concatenate(parts, 1))):
                out[s * (SUB // 2) + p] = value


def product(high, low, wh, wl, dims):
    both = lax.dot_general(jnp.concatenate([high, low], 0), wh, dims, preferred_element_type=F32)
    third = lax.dot_general(high, wl, dims, preferred_element_type=F32)
    return both[: high.shape[0]] + both[high.shape[0] :] + third


def three(value):
    parts = []
    for _ in range(3):
        parts.append(value.astype(BF16))
        value = value - parts[-1].astype(F32)
    return parts


def exact_gram(value):
    parts = jnp.concatenate(three(value), 0)
    out = lax.dot_general(parts, parts, NT, preferred_element_type=F32)
    rows = value.shape[0]
    blocks = [[out[rows * i : rows * i + rows, rows * j : rows * j + rows] for j in range(3)] for i in range(3)]
    small = (blocks[1][1] + (blocks[0][2] + blocks[2][0])) + (blocks[1][2] + blocks[2][1])
    return blocks[0][0] + ((blocks[0][1] + blocks[1][0]) + small)


def exact_weights(weights):
    high, mid, low = three(weights)
    zero = jnp.zeros_like(high)
    lines = ([high] * 3, [mid, mid, zero], [low, zero, zero])
    return jnp.concatenate([jnp.concatenate(line, 1) for line in lines], 0)


def exact_combination(weights, value):
    out = lax.dot_general(weights, jnp.concatenate(three(value), 0), NN, preferred_element_type=F32)
    rows = weights.shape[0] // 3
    return out[:rows] + (out[rows : 2 * rows] + out[2 * rows :])


def spread_rows(bands, uh, ul, base, acc, s):
    wh, wl = (stage_weights(*bands(s, i), True) for i in range(2))
    start = (s - base) * 8
    high = uh[pl.ds(start, 8)].reshape(128, 2 * LANES)
    low = ul[pl.ds(start, 8)].reshape(128, 2 * LANES)
    for t in range(5):
        out = product(high, low, wh[t], wl[t], NN).reshape(8, 16, 2 * LANES)
        acc[pl.ds(s * 8 + 4 - t, 8)] += out


def gather_rows(bands, vh, vl, s):
    wh, wl = (stage_weights(*bands(s, i), False) for i in range(2))
    total = None
    for t in range(5):
        high = vh[pl.ds(s * 8 + t, 8)].reshape(128, 2 * LANES)
        low = vl[pl.ds(s * 8 + t, 8)].reshape(128, 2 * LANES)
        out = product(high, low, wh[t], wl[t], NT)
        total = out if total is None else total + out
    return total.reshape(8, 16, 2 * LANES)


def halves(value):
    return jnp.where(
        lane_iota(16) < LANES // 2,
        pltpu.roll(value[:, :LANES], LANES - HALO, 1),
        pltpu.roll(value[:, LANES:], HALO, 1),
    )


def join_kernel(halo, tags, out):
    out[...] = halo[...]
    out[halo.shape[0] - 1, 8:16, :] = tags[0:8, :]


def slots_of(tiles):
    return [(ref, index) for ref in tiles for index in range(ref.shape[0])]


def near_kernel(rows, xor, ntiles, taps_ref, radius_ref, labels, halo, *refs):
    tiles = slots_of(refs[:ntiles])
    bth, btl, acc, acc1, real_ref, base_ref, uh, ul, vh, vl = refs[ntiles:]
    where = Rows(rows, xor)
    blocks = [where.block(k) for k in range(len(tiles))]
    high, low, shift = tables(taps_ref, radius_ref)
    real_ref[...] = jnp.broadcast_to(shift, real_ref.shape)
    lines = [labels[j : j + 1, :] for j in range(len(tiles))]
    make_bands(where, blocks, high, low, lines, halo, base_ref, bth, btl)
    make_window(where, blocks, tiles, halo, uh, ul)
    acc[...] = jnp.zeros_like(acc)
    bands = lambda s, i: ((bth, btl)[i], s)
    where.each(lambda s: spread_rows(bands, uh, ul, 0, acc, s), len(tiles))
    if xor:
        blank = jnp.zeros((2, 16, 2 * LANES), BF16)
        for ref in (vh, vl):
            ref[0:2] = blank
        for ref, value in zip((vh, vl), split(acc[2:12] * where.inside()[None])):
            ref[2:12] = value
        for ref, value in zip((uh, ul), split(gather_rows(bands, vh, vl, 0))):
            ref[0:8] = value
        acc1[...] = jnp.zeros_like(acc1)
        spread_rows(bands, uh, ul, 0, acc1, 0)


def main_kernel(rows, xor, ndev, ntiles, taps_ref, radius_ref, real_ref, nbh, nbl, nacc, nacc1, *refs):
    if ntiles:
        halo = refs[0]
        tiles = slots_of(refs[1 : 1 + ntiles])
        refs = refs[1 + ntiles :]
    gram_ref, keep_ref, send_ref, uh, ul, fbh, fbl, base_ref, vh, vl, acc, kr, extra, copies, sems = refs
    where = Rows(rows, xor)
    pairs = rows * SUB // 2
    near = nbh.shape[0]
    shift = real_ref[0:1, :]
    shift = jnp.concatenate([shift, shift], 1)

    def bands(s, i):
        if xor and s >= near:
            return (fbh, fbl)[i], s - near
        return (nbh, nbl)[i], s

    blank = jnp.zeros((2, 16, 2 * LANES), BF16)
    for ref in (vh, vl):
        ref[0:2] = blank
        ref[pairs + 2 : pairs + 4] = blank
    inside = where.inside()

    acc[0 : near * 8 + 4] = nacc[...]
    if ntiles:
        acc[near * 8 + 4 :] = jnp.zeros((pairs - near * 8, 16, 2 * LANES), F32)
        blocks = [where.block(near + k) - near for k in range(len(tiles))]
        high, low, _ = tables(taps_ref, radius_ref)
        lines = [halo[halo.shape[0] - 1, 8 + j : 9 + j, :] for j in range(ntiles)]
        make_bands(where, blocks, high, low, lines, halo, base_ref, fbh, fbl)
        make_window(where, blocks, tiles, halo, uh, ul)
        for s in range(near, rows):
            spread_rows(bands, uh, ul, near, acc, s)

    def finish(n, count):
        def body(s):
            start = s * 8
            value = acc[pl.ds(start + 2, 8)]
            if n > 0:
                value = value - shift * kr[n - 1, pl.ds(start, 8)]
            value = value * inside[None]
            kr[n, pl.ds(start, 8)] = value
            high, low = split(value)
            vh[pl.ds(start + 2, 8)] = high
            vl[pl.ds(start + 2, 8)] = low

        where.each(body, count)

    def forward(first, count, last):
        def body(s):
            total = gather_rows(bands, vh, vl, s)
            if last:
                kr[NB - 1, pl.ds(s * 8, 8)] = total
            for ref, value in zip((uh, ul), split(total)):
                ref[pl.ds(s * 8, 8)] = value

        where.each(body, count, first)

    fewer = rows - 1
    finish(0, rows)
    for n, first, into, out in ((1, 1, rows, rows), (2, 0, fewer, fewer)):
        forward(first, into, False)
        if n == 1 and xor:
            acc[0:12] = nacc1[...]
            acc[12:] = jnp.zeros((pairs - 8, 16, 2 * LANES), F32)
        else:
            acc[...] = jnp.zeros_like(acc)
        where.each(lambda s: spread_rows(bands, uh, ul, 0, acc, s), into, first)
        finish(n, out)
    forward(0, fewer, True)

    for side, (ref, row) in enumerate(zip((keep_ref, send_ref), where.own())):
        for n in range(NB):
            for p in range(8):
                value = halves(kr[n, row * 8 + p])
                if n < NB - 1:
                    ref[n, p] = value
                else:
                    extra[side, p] = value
    gram = jnp.zeros((NB * 16, NB * 16), F32)
    for p in range(8):
        stack = [
            jnp.concatenate([ref[n, p] for n in range(NB - 1)] + [extra[side, p]], 0)
            for side, ref in enumerate((keep_ref, send_ref))
        ]
        stack = jnp.concatenate(stack, 1)
        gram = gram + exact_gram(stack)
    gram = jnp.concatenate([gram, jnp.zeros_like(gram)], 1)
    lanes, sub = lane_iota(16), lax.broadcasted_iota(jnp.int32, (16, LANES), 0)
    rel = lanes & 15

    def moved(i, j, a):
        return pltpu.roll(gram[16 * i : 16 * i + 16], (16 * (a - j)) % LANES, 1)

    message = jnp.zeros((16, LANES), F32)
    for a in range(NB - 1):
        even = moved(a, a, a)
        odd = moved(a, a + 1, a) if a < NB - 2 else moved(a + 1, a + 1, a) - shift[:, :LANES] * even
        here = lanes >> 4 == a
        message = jnp.where(here, jnp.where(sub >= rel, even, odd), message)
        corner = jnp.sum(jnp.where(here & (sub == rel), odd, 0.0), axis=1, keepdims=True)
        message = jnp.where(lanes == 48 + a, corner, message)
    message = jnp.where(lanes[:8] < LANES // 2, message[:8], pltpu.roll(message[8:], LANES // 2, 1))
    share = copies.shape[0]
    for dev in range(share):
        copies[dev] = message
    moves = [
        pltpu.make_async_copy(copies, gram_ref.at[pl.ds(i * share, share)], sems.at[i])
        for i in range(ndev // share)
    ]
    for move in moves:
        move.start()
    for move in moves:
        move.wait()


def last_kernel(rows, xor, real_ref, nbh, nbl, fbh, fbl, uh, ul, keep_ref, send_ref, keep3, send3, acc):
    where = Rows(rows, xor)
    near = nbh.shape[0]
    acc[...] = jnp.zeros_like(acc)
    bands = lambda s, i: ((nbh, nbl)[i], s)
    where.each(lambda s: spread_rows(bands, uh, ul, 0, acc, s), near)
    if xor:
        wh, wl = (stage_weights(ref, 0, True) for ref in (fbh, fbl))
        high = uh[near * 8 : near * 8 + 2].reshape(32, 2 * LANES)
        low = ul[near * 8 : near * 8 + 2].reshape(32, 2 * LANES)
        for t in (3, 4):
            out = product(high, low, wh[t], wl[t], NN).reshape(2, 16, 2 * LANES)
            acc[near * 8 + 4 - t : near * 8 + 6 - t] += out
    for ref, old, row in zip((keep3, send3), (keep_ref, send_ref), where.own()):
        for p in range(8):
            ref[p] = halves(acc[row * 8 + 2 + p]) - real_ref[0:1, :] * old[NB - 2, p]


def final_kernel(
    ndev, xor, real_ref, gram_ref, keep_ref, keep3, other_ref, other3, solution_ref, residual_ref
):
    r, q, _ = place()
    damp = real_ref[0:1, :] + 0.25 * DAMPING
    parts = [gram_ref[dev] for dev in range(ndev)]
    while len(parts) > 1:
        parts = [a + b for a, b in zip(parts[::2], parts[1::2])]
    lanes, sub = lane_iota(16), lax.broadcasted_iota(jnp.int32, (16, LANES), 0)
    shared = jnp.concatenate([parts[0], pltpu.roll(parts[0], LANES // 2, 1)], 0)
    turned = jnp.concatenate([shared] + [jnp.zeros_like(shared)] * 7, 0).T
    grams = []
    for a in range(NB - 1):
        block = pltpu.roll(shared, LANES - 16 * a, 1) if a else shared
        other = turned[16 * a : 16 * a + 16]
        corner = shared[:, 48 + a : 49 + a]
        grams.append(jnp.where(sub >= lanes, block, other))
        grams.append(jnp.where(sub < lanes, block, jnp.where(sub == lanes, corner, other)))

    def at(g, place):
        return pltpu.roll(grams[g], 16 * place, 1) if place else grams[g]

    def line_of(entry):
        line = jnp.zeros((16, LANES), F32)
        for j in range(3):
            line = jnp.where(lanes >> 4 == j, entry(j), line)
        return line

    lines = [line_of(lambda j: at(i + j + 1, j) + damp * at(i + j, j)) for i in range(3)]
    matrix = jnp.concatenate(lines + [line_of(lambda j: at(j, j))], 0)
    lane = lane_iota(1)
    for panel in range(6):
        spread = [
            jnp.broadcast_to(matrix[:, 8 * panel + i : 8 * panel + i + 1], (64, LANES)) for i in range(8)
        ]
        for i in range(8):
            k = 8 * panel + i
            column = spread[i]
            scaled = column * (1.0 / column[k : k + 1, :])
            matrix = matrix - scaled * (matrix[k : k + 1, :] - (lane == k).astype(F32))
            for j in range(i + 1, 8):
                m = 8 * panel + j
                spread[j] = spread[j] - scaled * column[m : m + 1, :]
    c = jnp.where(lanes < 48, matrix[48:], 0.0)
    eye = (sub == lanes).astype(F32)
    weights = jnp.concatenate([0.5 * c, 2.0 * (eye - damp * c - pltpu.roll(c, 16, 1))], 0)[:, : NB * 16]
    weights = exact_weights(weights)
    down = r >> 1
    first = lanes < LANES // 2
    first2 = jnp.concatenate([first, first], 0)
    outs = (
        solution_ref.reshape(16 * SUB, LANES),
        residual_ref.reshape(16 * SUB, LANES),
    )
    for p in range(8):
        at = p + down * (7 - 2 * p) if xor else p
        mine = jnp.concatenate([keep_ref[n, at] for n in range(NB - 1)] + [keep3[at]], 0)
        pair = jnp.concatenate([other_ref[n, at] for n in range(NB - 1)] + [other3[at]], 0)
        both = jnp.concatenate([mine, pair], 1)
        out = exact_combination(weights, both)
        a, b = out[:, :LANES], out[:, LANES:]
        left, right = jnp.where(q == 0, a, b), jnp.where(q == 0, b, a)
        even = jnp.where(first2, left, pltpu.roll(right, LANES // 2, 1))
        odd = jnp.where(first2, pltpu.roll(left, LANES // 2, 1), right)
        if xor:
            even, odd = jnp.where(down > 0, odd, even), jnp.where(down > 0, even, odd)
        for i, line in ((2 * p, even), (2 * p + 1, odd)):
            for o, ref in enumerate(outs):
                ref[pl.ds(i, 16, stride=SUB), :] = line[16 * o : 16 * o + 16]


def per_device(measured, regions, kernels, radius):
    nrow, ncol = lax.axis_size("row"), lax.axis_size("col")
    ndev = nrow * ncol
    def flip(value, bit):
        return lax.ppermute(value, "row", [(i, i ^ bit) for i in range(nrow)])

    facing = []
    for i in range(nrow):
        for j in range(ncol):
            other = j + (1 if (i ^ j) & 1 else -1)
            if 0 <= other < ncol:
                facing.append((i * ncol + j, i * ncol + other))

    def call(kernel, name, out, operands, scratch, mib, specs=None):
        return pl.pallas_call(
            kernel,
            out_shape=[jax.ShapeDtypeStruct(shape, kind) for shape, kind in out],
            in_specs=[VMEM] * len(operands),
            out_specs=specs or [VMEM] * len(out),
            scratch_shapes=[pltpu.VMEM(*s) if isinstance(s, tuple) else s for s in scratch],
            compiler_params=params(mib),
            name=name,
        )(*operands)

    def bands_of(count):
        return ((count, K, LANES, LANES), BF16)

    def rows_of(count, kind):
        return ((count, 16, 2 * LANES), kind)

    def bases_of(count):
        return ((count, K, 8, LANES), F32)

    def edges_of(count):
        return ((count * (SUB // PACK), 16, LANES), F32)

    xor = nrow == 4
    if xor:
        mine = measured[None]
        tiles = [mine, flip(mine, 1)]
        labels = [regions, flip(regions, 1)]
        over = flip(mine, 2)
    else:
        tiles = [lax.all_gather(measured, "row", axis=0)]
        labels = [lax.all_gather(regions, "row", axis=0, tiled=True)]
    near, pairs = sum(t.shape[0] for t in tiles), nrow * SUB // 2
    edges, reach = call(
        first_kernel,
        "first",
        [edges_of(tiles[0].shape[0]), ((8, LANES), jnp.int32)],
        [tiles[0], radius[None]],
        [],
        4,
    )
    slots = edges_of(near)[0][0] + 1
    edges, tags = call(
        functools.partial(pack_kernel, len(labels)),
        "pack",
        [((slots, 16, LANES), F32), ((16, LANES), F32)],
        [edges, *labels, *tiles[1:]],
        [],
        4,
    )
    halo = lax.ppermute(edges, ("row", "col"), facing)
    taps = jnp.transpose(kernels, (1, 2, 0))
    nbh, nbl, nacc, nacc1, real = call(
        functools.partial(near_kernel, nrow, xor, len(tiles)),
        "near",
        [bands_of(near)] * 2 + [rows_of(near * 8 + 4, F32), rows_of(12, F32), ((8, LANES), F32)],
        [taps, reach, tags, halo, *tiles],
        [bases_of(near)] + [rows_of(near * 8, BF16)] * 2 + [rows_of(12, BF16)] * 2,
        8 + 2 * nrow,
    )
    far, ntiles = [], 0
    if xor:
        over, halo = lax.optimization_barrier((over, halo))
        (joined,) = call(join_kernel, "join", [((slots, 16, LANES), F32)], [halo, tags], [], 4)
        far, ntiles = [flip(joined, 2), over, flip(over, 1)], 2
    packed = ((NB - 1, 8, 16, LANES), F32)
    extra = max(nrow - near, 1)
    share = max(ndev // 8, 1)
    out = [((ndev, 8, LANES), F32), packed, packed] + [rows_of(pairs, BF16)] * 2 + [bands_of(extra)] * 2
    grams, keep, send, uh, ul, fbh, fbl = call(
        functools.partial(main_kernel, nrow, xor, ndev, ntiles),
        "krylov",
        out,
        [taps, reach, real, nbh, nbl, nacc, nacc1, *far],
        [bases_of(extra)]
        + [rows_of(pairs + 4, BF16)] * 2
        + [rows_of(pairs + 4, F32), ((NB, pairs, 16, 2 * LANES), F32), ((2, 8, 16, LANES), F32)]
        + [((share, 8, LANES), F32), pltpu.SemaphoreType.DMA((ndev // share,))],
        8 + 3 * nrow,
        [pl.BlockSpec(memory_space=pl.ANY)] + [VMEM] * (len(out) - 1),
    )
    grams = lax.all_to_all(grams, ("row", "col"), 0, 0)
    single = ((8, 16, LANES), F32)
    keep3, send3 = call(
        functools.partial(last_kernel, nrow, xor),
        "last",
        [single, single],
        [real, nbh, nbl, fbh, fbl, uh, ul, keep, send],
        [rows_of(near * 8 + 4, F32)],
        8 + 2 * nrow,
    )
    send, send3 = lax.optimization_barrier((send, send3))
    tile = ((16, SUB, LANES), F32)
    return tuple(
        call(
            functools.partial(final_kernel, ndev, xor),
            "combine",
            [tile, tile],
            [real, grams, keep, keep3, flip(send, 1), flip(send3, 1)],
            [],
            8,
        )
    )


def solution(mesh):
    in_specs = (P(None, "row", "col"), P("row", "col"), P(), P())
    out_specs = (P(None, "row", "col"), P(None, "row", "col"))
    return jax.shard_map(
        per_device, mesh=mesh, in_specs=in_specs, out_specs=out_specs, check_vma=False
    )
```

```python
import functools

import jax
import jax.numpy as jnp
from jax import lax
from jax.experimental import pallas as pl
from jax.experimental.pallas import tpu as pltpu
from jax.sharding import PartitionSpec as P

R = 4
K = 9
SUB = 16
REG = 64
DAMPING = 0.1

LANES = 128
HALO = 32
PACK = LANES // HALO
NB = 4

F32 = jnp.float32
BF16 = jnp.bfloat16
NN = (((1,), (0,)), ((), ()))
NT = (((1,), (1,)), ((), ()))
VMEM = pl.BlockSpec(memory_space=pltpu.VMEM)
SMEM = pl.BlockSpec(memory_space=pltpu.SMEM)
def params(mib):
    return pltpu.CompilerParams(vmem_limit_bytes=mib << 20)


def split(value):
    high = value.astype(BF16)
    return high, (value - high.astype(F32)).astype(BF16)


def lane_iota(rows):
    return lax.broadcasted_iota(jnp.int32, (rows, LANES), 1)


def row_of(ref, index, row):
    frames, rows = ref.shape[1], ref.shape[2]
    flat = ref.reshape(ref.shape[0] * frames * rows, LANES)
    return flat[pl.ds(index * frames * rows + row, frames, stride=rows), :]


def place():
    r, c = lax.axis_index("row"), lax.axis_index("col")
    q = (r ^ c) & 1
    beside = jnp.where(q == 0, c > 0, c < lax.axis_size("col") - 1)
    return r, q, beside.astype(jnp.int32)


def pack_tile(tile, index, out, slot):
    q = place()[1]
    for group in range(SUB // PACK):
        packed = None
        for m in range(PACK):
            line = row_of(tile, index, group * PACK + m)
            line = pltpu.roll(line, HALO * m + HALO * q, 1)
            lanes = lane_iota(line.shape[0])
            packed = line if packed is None else jnp.where(lanes >= HALO * m, line, packed)
        out[slot + group] = packed


def first_kernel(tile, radius_ref, out, reach_ref):
    for index in range(tile.shape[0]):
        pack_tile(tile, index, out, index * (SUB // PACK))
    reach_ref[...] = jnp.zeros_like(reach_ref)
    reach_ref[0:1, :REG] = radius_ref[...]


def pack_kernel(nlabels, packed, *refs):
    labels, tiles, (out, tags) = refs[:nlabels], refs[nlabels:-2], refs[-2:]
    slot = packed.shape[0]
    out[:slot] = packed[...]
    for tile in tiles:
        pack_tile(tile, 0, out, slot)
        slot += SUB // PACK
    tags[...] = jnp.zeros((16, LANES), F32)
    line = 0
    for ref in labels:
        height, width = ref.shape
        tags[line : line + height, :width] = (ref[...] + 1).astype(F32)
        line += height
    out[slot] = tags[...]


def stage_weights(bt, s, transposed):
    zero = jnp.zeros((LANES, LANES), BF16)

    def block(a):
        return bt[s, a] if 0 <= a < K else zero

    blocks = []
    for t in range(5):
        if transposed:
            index = [[2 * t + i - o for o in range(2)] for i in range(2)]
        else:
            index = [[8 - 2 * t + o - i for i in range(2)] for o in range(2)]
        blocks.append(
            jnp.concatenate([jnp.concatenate([block(a) for a in line], 1) for line in index], 0)
        )
    return blocks


class Rows:
    def __init__(self, rows, xor):
        self.rows, self.xor = rows, xor
        self.r, self.q, self.beside = place()
        self.down = (self.r >> 1) if xor else 0
        lanes = lane_iota(16)
        start = (LANES - HALO) * self.q
        self.in_halo = (lanes >= start) & (lanes < start + HALO)

    def block(self, k):
        return (k & 2) + ((k ^ self.r ^ self.down) & 1) if self.xor else k

    def turn(self, i, last):
        return i + self.down * (last - 2 * i) if self.xor else i

    def each(self, body, count, first=0):
        if self.xor:
            for s in range(first, count):
                body(s)
        else:
            lax.fori_loop(0, self.rows, lambda s, c: (body(s), c)[1], 0)

    def inside(self):
        mask = jnp.where(self.in_halo, self.beside.astype(F32), 1.0)
        return jnp.concatenate([mask, mask], 1)

    def own(self):
        return (self.block(0), self.block(1)) if self.xor else (self.r, self.r ^ 1)


def tables(taps_ref, radius_ref):
    radius = radius_ref[0:1, :REG]
    high, low, total = [], [], jnp.zeros((1, REG), F32)
    b = lax.broadcasted_iota(jnp.int32, (K, REG), 0)
    for a in range(K):
        reach = jnp.maximum(jnp.abs(b - R), abs(a - R))
        taps = jnp.where(reach <= radius, 0.5 * taps_ref[a], 0.0)
        total = total + jnp.sum(taps, axis=0, keepdims=True)
        for part, value in zip((high, low), split(taps)):
            part.append(value)
    squares = total * total
    mean = jnp.sum(squares, axis=1, keepdims=True) * (1.0 / REG)
    return high, low, 0.5 * jnp.sqrt(mean * jnp.max(squares, axis=1, keepdims=True))


def make_bands(where, blocks, high, low, labels, halo, base_ref, bth, btl):
    lanes = lane_iota(8)
    count = len(blocks)
    hots = []
    for j in range(count):
        own = jnp.broadcast_to(labels[j], (8, LANES))
        beside = jnp.broadcast_to(halo[count * (SUB // PACK) + j // 16, j % 16 : j % 16 + 1, :], (8, LANES))
        left = jnp.where(lanes < 2, pltpu.roll(beside, LANES - 6, 1), pltpu.roll(own, 2, 1))
        right = jnp.where(lanes < 6, pltpu.roll(own, LANES - 2, 1), pltpu.roll(beside, 6, 1))
        window = jnp.where(where.q == 0, left, right)
        diagonal = lanes == lax.broadcasted_iota(jnp.int32, (8, LANES), 0)
        column = jnp.sum(jnp.where(diagonal, window, 0.0), axis=1, keepdims=True)
        hots.append((column == (lanes[:, :REG] + 1).astype(F32)).astype(F32))
    hot = jnp.concatenate(hots, 0).astype(BF16)
    b = lax.broadcasted_iota(jnp.int32, (K, LANES), 0)
    spread = (lax.broadcasted_iota(jnp.int32, (K, LANES), 1) == (LANES + R - b) % LANES).astype(BF16)
    for a in range(K):
        base = None
        for part in (high, low):
            picked = lax.dot_general(hot, part[a], NT, preferred_element_type=F32).astype(BF16)
            line = lax.dot_general(picked, spread, NN, preferred_element_type=F32)
            base = line if base is None else base + line
        for j in range(count):
            base_ref[j, a] = base[8 * j : 8 * j + 8]
    for j, s in enumerate(blocks):
        for a in range(K):
            squares = base_ref[j, where.turn(a, K - 1)]
            for c in range(LANES // SUB):
                band = jnp.broadcast_to(squares[c : c + 1], (SUB, LANES))
                band = pltpu.roll(band, SUB * c, 1, stride=1, stride_axis=0)
                for ref, value in zip((bth, btl), split(band)):
                    ref[s, a, c * SUB : (c + 1) * SUB, :] = value


def make_window(where, blocks, tiles, halo, uh, ul):
    for j, (s, (ref, index)) in enumerate(zip(blocks, tiles)):
        for p in range(SUB // 2):
            parts = []
            for row in (2 * p, 2 * p + 1):
                i = where.turn(row, SUB - 1)
                line = row_of(ref, index, row)
                if where.xor:
                    line = jnp.where(where.down > 0, row_of(ref, index, SUB - 1 - row), line)
                line = pltpu.roll(line, HALO + (LANES - 2 * HALO) * where.q, 1)
                edge = halo[j * (SUB // PACK) + i // PACK]
                edge = pltpu.roll(edge, (LANES - HALO * (i % PACK) + (LANES - HALO) * where.q) % LANES, 1)
                parts.append(jnp.where(where.in_halo, edge, line))
            for out, value in zip((uh, ul), split(jnp.concatenate(parts, 1))):
                out[s * (SUB // 2) + p] = value


def product(high, low, wh, wl, dims):
    both = lax.dot_general(jnp.concatenate([high, low], 0), wh, dims, preferred_element_type=F32)
    third = lax.dot_general(high, wl, dims, preferred_element_type=F32)
    return both[: high.shape[0]] + both[high.shape[0] :] + third


def three(value):
    parts = []
    for _ in range(3):
        parts.append(value.astype(BF16))
        value = value - parts[-1].astype(F32)
    return parts


def exact_gram(value):
    parts = jnp.concatenate(three(value), 0)
    out = lax.dot_general(parts, parts, NT, preferred_element_type=F32)
    rows = value.shape[0]
    blocks = [[out[rows * i : rows * i + rows, rows * j : rows * j + rows] for j in range(3)] for i in range(3)]
    small = (blocks[1][1] + (blocks[0][2] + blocks[2][0])) + (blocks[1][2] + blocks[2][1])
    return blocks[0][0] + ((blocks[0][1] + blocks[1][0]) + small)


def exact_weights(weights):
    high, mid, low = three(weights)
    zero = jnp.zeros_like(high)
    lines = ([high] * 3, [mid, mid, zero], [low, zero, zero])
    return jnp.concatenate([jnp.concatenate(line, 1) for line in lines], 0)


def exact_combination(weights, value):
    out = lax.dot_general(weights, jnp.concatenate(three(value), 0), NN, preferred_element_type=F32)
    rows = weights.shape[0] // 3
    return out[:rows] + (out[rows : 2 * rows] + out[2 * rows :])


def spread_rows(bands, uh, ul, base, acc, s):
    wh, wl = (stage_weights(*bands(s, i), True) for i in range(2))
    start = (s - base) * 8
    high = uh[pl.ds(start, 8)].reshape(128, 2 * LANES)
    low = ul[pl.ds(start, 8)].reshape(128, 2 * LANES)
    for t in range(5):
        out = product(high, low, wh[t], wl[t], NN).reshape(8, 16, 2 * LANES)
        acc[pl.ds(s * 8 + 4 - t, 8)] += out


def gather_rows(bands, vh, vl, s):
    wh, wl = (stage_weights(*bands(s, i), False) for i in range(2))
    total = None
    for t in range(5):
        high = vh[pl.ds(s * 8 + t, 8)].reshape(128, 2 * LANES)
        low = vl[pl.ds(s * 8 + t, 8)].reshape(128, 2 * LANES)
        out = product(high, low, wh[t], wl[t], NT)
        total = out if total is None else total + out
    return total.reshape(8, 16, 2 * LANES)


def halves(value):
    return jnp.where(
        lane_iota(16) < LANES // 2,
        pltpu.roll(value[:, :LANES], LANES - HALO, 1),
        pltpu.roll(value[:, LANES:], HALO, 1),
    )


def join_kernel(halo, tags, out):
    out[...] = halo[...]
    out[halo.shape[0] - 1, 8:16, :] = tags[0:8, :]


def slots_of(tiles):
    return [(ref, index) for ref in tiles for index in range(ref.shape[0])]


def near_kernel(rows, xor, ntiles, taps_ref, radius_ref, labels, halo, *refs):
    tiles = slots_of(refs[:ntiles])
    bth, btl, acc, acc1, real_ref, base_ref, uh, ul, vh, vl = refs[ntiles:]
    where = Rows(rows, xor)
    blocks = [where.block(k) for k in range(len(tiles))]
    high, low, shift = tables(taps_ref, radius_ref)
    real_ref[...] = jnp.broadcast_to(shift, real_ref.shape)
    lines = [labels[j : j + 1, :] for j in range(len(tiles))]
    make_bands(where, blocks, high, low, lines, halo, base_ref, bth, btl)
    make_window(where, blocks, tiles, halo, uh, ul)
    acc[...] = jnp.zeros_like(acc)
    bands = lambda s, i: ((bth, btl)[i], s)
    where.each(lambda s: spread_rows(bands, uh, ul, 0, acc, s), len(tiles))
    if xor:
        blank = jnp.zeros((2, 16, 2 * LANES), BF16)
        for ref in (vh, vl):
            ref[0:2] = blank
        for ref, value in zip((vh, vl), split(acc[2:12] * where.inside()[None])):
            ref[2:12] = value
        for ref, value in zip((uh, ul), split(gather_rows(bands, vh, vl, 0))):
            ref[0:8] = value
        acc1[...] = jnp.zeros_like(acc1)
        spread_rows(bands, uh, ul, 0, acc1, 0)


def main_kernel(rows, xor, ndev, ntiles, taps_ref, radius_ref, real_ref, nbh, nbl, nacc, nacc1, *refs):
    if ntiles:
        halo = refs[0]
        tiles = slots_of(refs[1 : 1 + ntiles])
        refs = refs[1 + ntiles :]
    gram_ref, keep_ref, send_ref, uh, ul, fbh, fbl, base_ref, vh, vl, acc, kr, extra, copies, sems = refs
    where = Rows(rows, xor)
    pairs = rows * SUB // 2
    near = nbh.shape[0]
    shift = real_ref[0:1, :]
    shift = jnp.concatenate([shift, shift], 1)

    def bands(s, i):
        if xor and s >= near:
            return (fbh, fbl)[i], s - near
        return (nbh, nbl)[i], s

    blank = jnp.zeros((2, 16, 2 * LANES), BF16)
    for ref in (vh, vl):
        ref[0:2] = blank
        ref[pairs + 2 : pairs + 4] = blank
    inside = where.inside()

    acc[0 : near * 8 + 4] = nacc[...]
    if ntiles:
        acc[near * 8 + 4 :] = jnp.zeros((pairs - near * 8, 16, 2 * LANES), F32)
        blocks = [where.block(near + k) - near for k in range(len(tiles))]
        high, low, _ = tables(taps_ref, radius_ref)
        lines = [halo[halo.shape[0] - 1, 8 + j : 9 + j, :] for j in range(ntiles)]
        make_bands(where, blocks, high, low, lines, halo, base_ref, fbh, fbl)
        make_window(where, blocks, tiles, halo, uh, ul)
        for s in range(near, rows):
            spread_rows(bands, uh, ul, near, acc, s)

    def finish(n, count):
        def body(s):
            start = s * 8
            value = acc[pl.ds(start + 2, 8)]
            if n > 0:
                value = value - shift * kr[n - 1, pl.ds(start, 8)]
            value = value * inside[None]
            kr[n, pl.ds(start, 8)] = value
            high, low = split(value)
            vh[pl.ds(start + 2, 8)] = high
            vl[pl.ds(start + 2, 8)] = low

        where.each(body, count)

    def forward(first, count, last):
        def body(s):
            total = gather_rows(bands, vh, vl, s)
            if last:
                kr[NB - 1, pl.ds(s * 8, 8)] = total
            for ref, value in zip((uh, ul), split(total)):
                ref[pl.ds(s * 8, 8)] = value

        where.each(body, count, first)

    fewer = rows - 1
    finish(0, rows)
    for n, first, into, out in ((1, 1, rows, rows), (2, 0, fewer, fewer)):
        forward(first, into, False)
        if n == 1 and xor:
            acc[0:12] = nacc1[...]
            acc[12:] = jnp.zeros((pairs - 8, 16, 2 * LANES), F32)
        else:
            acc[...] = jnp.zeros_like(acc)
        where.each(lambda s: spread_rows(bands, uh, ul, 0, acc, s), into, first)
        finish(n, out)
    forward(0, fewer, True)

    for side, (ref, row) in enumerate(zip((keep_ref, send_ref), where.own())):
        for n in range(NB):
            for p in range(8):
                value = halves(kr[n, row * 8 + p])
                if n < NB - 1:
                    ref[n, p] = value
                else:
                    extra[side, p] = value
    gram = jnp.zeros((NB * 16, NB * 16), F32)
    for p in range(8):
        stack = [
            jnp.concatenate([ref[n, p] for n in range(NB - 1)] + [extra[side, p]], 0)
            for side, ref in enumerate((keep_ref, send_ref))
        ]
        stack = jnp.concatenate(stack, 1)
        gram = gram + exact_gram(stack)
    gram = jnp.concatenate([gram, jnp.zeros_like(gram)], 1)
    lanes, sub = lane_iota(16), lax.broadcasted_iota(jnp.int32, (16, LANES), 0)
    rel = lanes & 15

    def moved(i, j, a):
        return pltpu.roll(gram[16 * i : 16 * i + 16], (16 * (a - j)) % LANES, 1)

    message = jnp.zeros((16, LANES), F32)
    for a in range(NB - 1):
        even = moved(a, a, a)
        odd = moved(a, a + 1, a) if a < NB - 2 else moved(a + 1, a + 1, a) - shift[:, :LANES] * even
        here = lanes >> 4 == a
        message = jnp.where(here, jnp.where(sub >= rel, even, odd), message)
        corner = jnp.sum(jnp.where(here & (sub == rel), odd, 0.0), axis=1, keepdims=True)
        message = jnp.where(lanes == 48 + a, corner, message)
    message = jnp.where(lanes[:8] < LANES // 2, message[:8], pltpu.roll(message[8:], LANES // 2, 1))
    share = copies.shape[0]
    for dev in range(share):
        copies[dev] = message
    moves = [
        pltpu.make_async_copy(copies, gram_ref.at[pl.ds(i * share, share)], sems.at[i])
        for i in range(ndev // share)
    ]
    for move in moves:
        move.start()
    for move in moves:
        move.wait()


def last_kernel(rows, xor, real_ref, nbh, nbl, fbh, fbl, uh, ul, keep_ref, send_ref, keep3, send3, acc):
    where = Rows(rows, xor)
    near = nbh.shape[0]
    acc[...] = jnp.zeros_like(acc)
    bands = lambda s, i: ((nbh, nbl)[i], s)
    where.each(lambda s: spread_rows(bands, uh, ul, 0, acc, s), near)
    if xor:
        wh, wl = (stage_weights(ref, 0, True) for ref in (fbh, fbl))
        high = uh[near * 8 : near * 8 + 2].reshape(32, 2 * LANES)
        low = ul[near * 8 : near * 8 + 2].reshape(32, 2 * LANES)
        for t in (3, 4):
            out = product(high, low, wh[t], wl[t], NN).reshape(2, 16, 2 * LANES)
            acc[near * 8 + 4 - t : near * 8 + 6 - t] += out
    for ref, old, row in zip((keep3, send3), (keep_ref, send_ref), where.own()):
        for p in range(8):
            ref[p] = halves(acc[row * 8 + 2 + p]) - real_ref[0:1, :] * old[NB - 2, p]


def final_kernel(
    ndev, xor, real_ref, gram_ref, keep_ref, keep3, other_ref, other3, solution_ref, residual_ref
):
    r, q, _ = place()
    damp = real_ref[0:1, :] + 0.25 * DAMPING
    parts = [gram_ref[dev] for dev in range(ndev)]
    while len(parts) > 1:
        parts = [a + b for a, b in zip(parts[::2], parts[1::2])]
    lanes, sub = lane_iota(16), lax.broadcasted_iota(jnp.int32, (16, LANES), 0)
    shared = jnp.concatenate([parts[0], pltpu.roll(parts[0], LANES // 2, 1)], 0)
    turned = jnp.concatenate([shared] + [jnp.zeros_like(shared)] * 7, 0).T
    grams = []
    for a in range(NB - 1):
        block = pltpu.roll(shared, LANES - 16 * a, 1) if a else shared
        other = turned[16 * a : 16 * a + 16]
        corner = shared[:, 48 + a : 49 + a]
        grams.append(jnp.where(sub >= lanes, block, other))
        grams.append(jnp.where(sub < lanes, block, jnp.where(sub == lanes, corner, other)))

    def at(g, place):
        return pltpu.roll(grams[g], 16 * place, 1) if place else grams[g]

    def line_of(entry):
        line = jnp.zeros((16, LANES), F32)
        for j in range(3):
            line = jnp.where(lanes >> 4 == j, entry(j), line)
        return line

    lines = [line_of(lambda j: at(i + j + 1, j) + damp * at(i + j, j)) for i in range(3)]
    matrix = jnp.concatenate(lines + [line_of(lambda j: at(j, j))], 0)
    lane = lane_iota(64)
    for panel in range(6):
        spread = [
            jnp.broadcast_to(matrix[:, 8 * panel + i : 8 * panel + i + 1], (64, LANES)) for i in range(8)
        ]
        for i in range(8):
            k = 8 * panel + i
            column = spread[i]
            scaled = column * (1.0 / column[k : k + 1, :])
            matrix = jnp.where(lane == k, scaled, matrix - scaled * matrix[k : k + 1, :])
            for j in range(i + 1, 8):
                m = 8 * panel + j
                spread[j] = spread[j] - scaled * column[m : m + 1, :]
    c = jnp.where(lanes < 48, matrix[48:], 0.0)
    eye = (sub == lanes).astype(F32)
    weights = jnp.concatenate([0.5 * c, 2.0 * (eye - damp * c - pltpu.roll(c, 16, 1))], 0)[:, : NB * 16]
    weights = exact_weights(weights)
    down = r >> 1
    first = lanes < LANES // 2
    first2 = jnp.concatenate([first, first], 0)
    outs = (
        solution_ref.reshape(16 * SUB, LANES),
        residual_ref.reshape(16 * SUB, LANES),
    )
    for p in range(8):
        at = p + down * (7 - 2 * p) if xor else p
        mine = jnp.concatenate([keep_ref[n, at] for n in range(NB - 1)] + [keep3[at]], 0)
        pair = jnp.concatenate([other_ref[n, at] for n in range(NB - 1)] + [other3[at]], 0)
        both = jnp.concatenate([mine, pair], 1)
        out = exact_combination(weights, both)
        a, b = out[:, :LANES], out[:, LANES:]
        left, right = jnp.where(q == 0, a, b), jnp.where(q == 0, b, a)
        even = jnp.where(first2, left, pltpu.roll(right, LANES // 2, 1))
        odd = jnp.where(first2, pltpu.roll(left, LANES // 2, 1), right)
        if xor:
            even, odd = jnp.where(down > 0, odd, even), jnp.where(down > 0, even, odd)
        for i, line in ((2 * p, even), (2 * p + 1, odd)):
            for o, ref in enumerate(outs):
                ref[pl.ds(i, 16, stride=SUB), :] = line[16 * o : 16 * o + 16]


def per_device(measured, regions, kernels, radius):
    nrow, ncol = lax.axis_size("row"), lax.axis_size("col")
    ndev = nrow * ncol
    def flip(value, bit):
        return lax.ppermute(value, "row", [(i, i ^ bit) for i in range(nrow)])

    facing = []
    for i in range(nrow):
        for j in range(ncol):
            other = j + (1 if (i ^ j) & 1 else -1)
            if 0 <= other < ncol:
                facing.append((i * ncol + j, i * ncol + other))

    def call(kernel, name, out, operands, scratch, mib, specs=None):
        return pl.pallas_call(
            kernel,
            out_shape=[jax.ShapeDtypeStruct(shape, kind) for shape, kind in out],
            in_specs=[VMEM] * len(operands),
            out_specs=specs or [VMEM] * len(out),
            scratch_shapes=[pltpu.VMEM(*s) if isinstance(s, tuple) else s for s in scratch],
            compiler_params=params(mib),
            name=name,
        )(*operands)

    def bands_of(count):
        return ((count, K, LANES, LANES), BF16)

    def rows_of(count, kind):
        return ((count, 16, 2 * LANES), kind)

    def bases_of(count):
        return ((count, K, 8, LANES), F32)

    def edges_of(count):
        return ((count * (SUB // PACK), 16, LANES), F32)

    xor = nrow == 4
    if xor:
        mine = measured[None]
        tiles = [mine, flip(mine, 1)]
        labels = [regions, flip(regions, 1)]
        over = flip(mine, 2)
    else:
        tiles = [lax.all_gather(measured, "row", axis=0)]
        labels = [lax.all_gather(regions, "row", axis=0, tiled=True)]
    near, pairs = sum(t.shape[0] for t in tiles), nrow * SUB // 2
    edges, reach = call(
        first_kernel,
        "first",
        [edges_of(tiles[0].shape[0]), ((8, LANES), jnp.int32)],
        [tiles[0], radius[None]],
        [],
        4,
    )
    slots = edges_of(near)[0][0] + 1
    edges, tags = call(
        functools.partial(pack_kernel, len(labels)),
        "pack",
        [((slots, 16, LANES), F32), ((16, LANES), F32)],
        [edges, *labels, *tiles[1:]],
        [],
        4,
    )
    halo = lax.ppermute(edges, ("row", "col"), facing)
    taps = jnp.transpose(kernels, (1, 2, 0))
    nbh, nbl, nacc, nacc1, real = call(
        functools.partial(near_kernel, nrow, xor, len(tiles)),
        "near",
        [bands_of(near)] * 2 + [rows_of(near * 8 + 4, F32), rows_of(12, F32), ((8, LANES), F32)],
        [taps, reach, tags, halo, *tiles],
        [bases_of(near)] + [rows_of(near * 8, BF16)] * 2 + [rows_of(12, BF16)] * 2,
        8 + 2 * nrow,
    )
    far, ntiles = [], 0
    if xor:
        over, halo = lax.optimization_barrier((over, halo))
        (joined,) = call(join_kernel, "join", [((slots, 16, LANES), F32)], [halo, tags], [], 4)
        far, ntiles = [flip(joined, 2), over, flip(over, 1)], 2
    packed = ((NB - 1, 8, 16, LANES), F32)
    extra = max(nrow - near, 1)
    share = max(ndev // 8, 1)
    out = [((ndev, 8, LANES), F32), packed, packed] + [rows_of(pairs, BF16)] * 2 + [bands_of(extra)] * 2
    grams, keep, send, uh, ul, fbh, fbl = call(
        functools.partial(main_kernel, nrow, xor, ndev, ntiles),
        "krylov",
        out,
        [taps, reach, real, nbh, nbl, nacc, nacc1, *far],
        [bases_of(extra)]
        + [rows_of(pairs + 4, BF16)] * 2
        + [rows_of(pairs + 4, F32), ((NB, pairs, 16, 2 * LANES), F32), ((2, 8, 16, LANES), F32)]
        + [((share, 8, LANES), F32), pltpu.SemaphoreType.DMA((ndev // share,))],
        8 + 3 * nrow,
        [pl.BlockSpec(memory_space=pl.ANY)] + [VMEM] * (len(out) - 1),
    )
    grams = lax.all_to_all(grams, ("row", "col"), 0, 0)
    single = ((8, 16, LANES), F32)
    keep3, send3 = call(
        functools.partial(last_kernel, nrow, xor),
        "last",
        [single, single],
        [real, nbh, nbl, fbh, fbl, uh, ul, keep, send],
        [rows_of(near * 8 + 4, F32)],
        8 + 2 * nrow,
    )
    send, send3 = lax.optimization_barrier((send, send3))
    tile = ((16, SUB, LANES), F32)
    return tuple(
        call(
            functools.partial(final_kernel, ndev, xor),
            "combine",
            [tile, tile],
            [real, grams, keep, keep3, flip(send, 1), flip(send3, 1)],
            [],
            8,
        )
    )


def solution(mesh):
    in_specs = (P(None, "row", "col"), P("row", "col"), P(), P())
    out_specs = (P(None, "row", "col"), P(None, "row", "col"))
    return jax.shard_map(
        per_device, mesh=mesh, in_specs=in_specs, out_specs=out_specs, check_vma=False
    )
```

```python
import functools

import jax
import jax.numpy as jnp
from jax import lax
from jax.experimental import pallas as pl
from jax.experimental.pallas import tpu as pltpu
from jax.sharding import PartitionSpec as P

R = 4
K = 9
SUB = 16
REG = 64
DAMPING = 0.1

LANES = 128
HALO = 32
PACK = LANES // HALO
NB = 4

F32 = jnp.float32
BF16 = jnp.bfloat16
NN = (((1,), (0,)), ((), ()))
NT = (((1,), (1,)), ((), ()))
VMEM = pl.BlockSpec(memory_space=pltpu.VMEM)
SMEM = pl.BlockSpec(memory_space=pltpu.SMEM)
def params(mib):
    return pltpu.CompilerParams(vmem_limit_bytes=mib << 20)


def split(value):
    high = value.astype(BF16)
    return high, (value - high.astype(F32)).astype(BF16)


def lane_iota(rows):
    return lax.broadcasted_iota(jnp.int32, (rows, LANES), 1)


def row_of(ref, index, row):
    frames, rows = ref.shape[1], ref.shape[2]
    flat = ref.reshape(ref.shape[0] * frames * rows, LANES)
    return flat[pl.ds(index * frames * rows + row, frames, stride=rows), :]


def place():
    r, c = lax.axis_index("row"), lax.axis_index("col")
    q = (r ^ c) & 1
    beside = jnp.where(q == 0, c > 0, c < lax.axis_size("col") - 1)
    return r, q, beside.astype(jnp.int32)


def pack_tile(tile, index, out, slot):
    q = place()[1]
    for group in range(SUB // PACK):
        packed = None
        for m in range(PACK):
            line = row_of(tile, index, group * PACK + m)
            line = pltpu.roll(line, HALO * m + HALO * q, 1)
            lanes = lane_iota(line.shape[0])
            packed = line if packed is None else jnp.where(lanes >= HALO * m, line, packed)
        out[slot + group] = packed


def first_kernel(tile, radius_ref, out, reach_ref):
    for index in range(tile.shape[0]):
        pack_tile(tile, index, out, index * (SUB // PACK))
    reach_ref[...] = jnp.zeros_like(reach_ref)
    reach_ref[0:1, :REG] = radius_ref[...]


def pack_kernel(nlabels, packed, *refs):
    labels, tiles, (out, tags) = refs[:nlabels], refs[nlabels:-2], refs[-2:]
    slot = packed.shape[0]
    out[:slot] = packed[...]
    for tile in tiles:
        pack_tile(tile, 0, out, slot)
        slot += SUB // PACK
    tags[...] = jnp.zeros((16, LANES), F32)
    line = 0
    for ref in labels:
        height, width = ref.shape
        tags[line : line + height, :width] = (ref[...] + 1).astype(F32)
        line += height
    out[slot] = tags[...]


def stage_weights(bt, s, transposed):
    zero = jnp.zeros((LANES, LANES), BF16)

    def block(a):
        return bt[s, a] if 0 <= a < K else zero

    blocks = []
    for t in range(5):
        if transposed:
            index = [[2 * t + i - o for o in range(2)] for i in range(2)]
        else:
            index = [[8 - 2 * t + o - i for i in range(2)] for o in range(2)]
        blocks.append(
            jnp.concatenate([jnp.concatenate([block(a) for a in line], 1) for line in index], 0)
        )
    return blocks


class Rows:
    def __init__(self, rows, xor):
        self.rows, self.xor = rows, xor
        self.r, self.q, self.beside = place()
        self.down = (self.r >> 1) if xor else 0
        lanes = lane_iota(16)
        start = (LANES - HALO) * self.q
        self.in_halo = (lanes >= start) & (lanes < start + HALO)

    def block(self, k):
        return (k & 2) + ((k ^ self.r ^ self.down) & 1) if self.xor else k

    def turn(self, i, last):
        return i + self.down * (last - 2 * i) if self.xor else i

    def each(self, body, count, first=0):
        if self.xor:
            for s in range(first, count):
                body(s)
        else:
            lax.fori_loop(0, self.rows, lambda s, c: (body(s), c)[1], 0)

    def inside(self):
        mask = jnp.where(self.in_halo, self.beside.astype(F32), 1.0)
        return jnp.concatenate([mask, mask], 1)

    def own(self):
        return (self.block(0), self.block(1)) if self.xor else (self.r, self.r ^ 1)


def tables(taps_ref, radius_ref):
    radius = radius_ref[0:1, :REG]
    high, low, total = [], [], jnp.zeros((1, REG), F32)
    b = lax.broadcasted_iota(jnp.int32, (K, REG), 0)
    for a in range(K):
        reach = jnp.maximum(jnp.abs(b - R), abs(a - R))
        taps = jnp.where(reach <= radius, 0.5 * taps_ref[a], 0.0)
        total = total + jnp.sum(taps, axis=0, keepdims=True)
        for part, value in zip((high, low), split(taps)):
            part.append(value)
    squares = total * total
    mean = jnp.sum(squares, axis=1, keepdims=True) * (1.0 / REG)
    return high, low, 0.5 * jnp.sqrt(mean * jnp.max(squares, axis=1, keepdims=True))


def make_bands(where, blocks, high, low, labels, halo, base_ref, bth, btl):
    lanes = lane_iota(8)
    count = len(blocks)
    hots = []
    for j in range(count):
        own = jnp.broadcast_to(labels[j], (8, LANES))
        beside = jnp.broadcast_to(halo[count * (SUB // PACK) + j // 16, j % 16 : j % 16 + 1, :], (8, LANES))
        left = jnp.where(lanes < 2, pltpu.roll(beside, LANES - 6, 1), pltpu.roll(own, 2, 1))
        right = jnp.where(lanes < 6, pltpu.roll(own, LANES - 2, 1), pltpu.roll(beside, 6, 1))
        window = jnp.where(where.q == 0, left, right)
        diagonal = lanes == lax.broadcasted_iota(jnp.int32, (8, LANES), 0)
        column = jnp.sum(jnp.where(diagonal, window, 0.0), axis=1, keepdims=True)
        hots.append((column == (lanes[:, :REG] + 1).astype(F32)).astype(F32))
    hot = jnp.concatenate(hots, 0).astype(BF16)
    b = lax.broadcasted_iota(jnp.int32, (K, LANES), 0)
    spread = (lax.broadcasted_iota(jnp.int32, (K, LANES), 1) == (LANES + R - b) % LANES).astype(BF16)
    for a in range(K):
        base = None
        for part in (high, low):
            picked = lax.dot_general(hot, part[a], NT, preferred_element_type=F32).astype(BF16)
            line = lax.dot_general(picked, spread, NN, preferred_element_type=F32)
            base = line if base is None else base + line
        for j in range(count):
            base_ref[j, a] = base[8 * j : 8 * j + 8]
    for j, s in enumerate(blocks):
        for a in range(K):
            squares = base_ref[j, where.turn(a, K - 1)]
            for c in range(LANES // SUB):
                band = jnp.broadcast_to(squares[c : c + 1], (SUB, LANES))
                band = pltpu.roll(band, SUB * c, 1, stride=1, stride_axis=0)
                for ref, value in zip((bth, btl), split(band)):
                    ref[s, a, c * SUB : (c + 1) * SUB, :] = value


def make_window(where, blocks, tiles, halo, uh, ul):
    for j, (s, (ref, index)) in enumerate(zip(blocks, tiles)):
        for p in range(SUB // 2):
            parts = []
            for row in (2 * p, 2 * p + 1):
                i = where.turn(row, SUB - 1)
                line = row_of(ref, index, row)
                if where.xor:
                    line = jnp.where(where.down > 0, row_of(ref, index, SUB - 1 - row), line)
                line = pltpu.roll(line, HALO + (LANES - 2 * HALO) * where.q, 1)
                edge = halo[j * (SUB // PACK) + i // PACK]
                edge = pltpu.roll(edge, (LANES - HALO * (i % PACK) + (LANES - HALO) * where.q) % LANES, 1)
                parts.append(jnp.where(where.in_halo, edge, line))
            for out, value in zip((uh, ul), split(jnp.concatenate(parts, 1))):
                out[s * (SUB // 2) + p] = value


def product(high, low, wh, wl, dims):
    both = lax.dot_general(jnp.concatenate([high, low], 0), wh, dims, preferred_element_type=F32)
    third = lax.dot_general(high, wl, dims, preferred_element_type=F32)
    return both[: high.shape[0]] + both[high.shape[0] :] + third


def three(value):
    parts = []
    for _ in range(3):
        parts.append(value.astype(BF16))
        value = value - parts[-1].astype(F32)
    return parts


def exact_gram(value):
    parts = jnp.concatenate(three(value), 0)
    out = lax.dot_general(parts, parts, NT, preferred_element_type=F32)
    rows = value.shape[0]
    blocks = [[out[rows * i : rows * i + rows, rows * j : rows * j + rows] for j in range(3)] for i in range(3)]
    small = (blocks[1][1] + (blocks[0][2] + blocks[2][0])) + (blocks[1][2] + blocks[2][1])
    return blocks[0][0] + ((blocks[0][1] + blocks[1][0]) + small)


def exact_weights(weights):
    high, mid, low = three(weights)
    zero = jnp.zeros_like(high)
    lines = ([high] * 3, [mid, mid, zero], [low, zero, zero])
    return jnp.concatenate([jnp.concatenate(line, 1) for line in lines], 0)


def exact_combination(weights, value):
    out = lax.dot_general(weights, jnp.concatenate(three(value), 0), NN, preferred_element_type=F32)
    rows = weights.shape[0] // 3
    return out[:rows] + (out[rows : 2 * rows] + out[2 * rows :])


def spread_rows(bands, uh, ul, base, acc, s):
    wh, wl = (stage_weights(*bands(s, i), True) for i in range(2))
    start = (s - base) * 8
    high = uh[pl.ds(start, 8)].reshape(128, 2 * LANES)
    low = ul[pl.ds(start, 8)].reshape(128, 2 * LANES)
    for t in range(5):
        out = product(high, low, wh[t], wl[t], NN).reshape(8, 16, 2 * LANES)
        acc[pl.ds(s * 8 + 4 - t, 8)] += out


def gather_rows(bands, vh, vl, s):
    wh, wl = (stage_weights(*bands(s, i), False) for i in range(2))
    total = None
    for t in range(5):
        high = vh[pl.ds(s * 8 + t, 8)].reshape(128, 2 * LANES)
        low = vl[pl.ds(s * 8 + t, 8)].reshape(128, 2 * LANES)
        out = product(high, low, wh[t], wl[t], NT)
        total = out if total is None else total + out
    return total.reshape(8, 16, 2 * LANES)


def halves(value):
    return jnp.where(
        lane_iota(16) < LANES // 2,
        pltpu.roll(value[:, :LANES], LANES - HALO, 1),
        pltpu.roll(value[:, LANES:], HALO, 1),
    )


def join_kernel(halo, tags, out):
    out[...] = halo[...]
    out[halo.shape[0] - 1, 8:16, :] = tags[0:8, :]


def slots_of(tiles):
    return [(ref, index) for ref in tiles for index in range(ref.shape[0])]


def near_kernel(rows, xor, ntiles, taps_ref, radius_ref, labels, halo, *refs):
    tiles = slots_of(refs[:ntiles])
    bth, btl, acc, acc1, real_ref, base_ref, uh, ul, vh, vl = refs[ntiles:]
    where = Rows(rows, xor)
    blocks = [where.block(k) for k in range(len(tiles))]
    high, low, shift = tables(taps_ref, radius_ref)
    real_ref[...] = jnp.broadcast_to(shift, real_ref.shape)
    lines = [labels[j : j + 1, :] for j in range(len(tiles))]
    make_bands(where, blocks, high, low, lines, halo, base_ref, bth, btl)
    make_window(where, blocks, tiles, halo, uh, ul)
    acc[...] = jnp.zeros_like(acc)
    bands = lambda s, i: ((bth, btl)[i], s)
    where.each(lambda s: spread_rows(bands, uh, ul, 0, acc, s), len(tiles))
    if xor:
        blank = jnp.zeros((2, 16, 2 * LANES), BF16)
        for ref in (vh, vl):
            ref[0:2] = blank
        for ref, value in zip((vh, vl), split(acc[2:12] * where.inside()[None])):
            ref[2:12] = value
        for ref, value in zip((uh, ul), split(gather_rows(bands, vh, vl, 0))):
            ref[0:8] = value
        acc1[...] = jnp.zeros_like(acc1)
        spread_rows(bands, uh, ul, 0, acc1, 0)


def main_kernel(rows, xor, ndev, ntiles, taps_ref, radius_ref, real_ref, nbh, nbl, nacc, nacc1, *refs):
    if ntiles:
        halo = refs[0]
        tiles = slots_of(refs[1 : 1 + ntiles])
        refs = refs[1 + ntiles :]
    gram_ref, keep_ref, send_ref, uh, ul, fbh, fbl, base_ref, vh, vl, acc, kr, extra, copies, sems = refs
    where = Rows(rows, xor)
    pairs = rows * SUB // 2
    near = nbh.shape[0]
    shift = real_ref[0:1, :]
    shift = jnp.concatenate([shift, shift], 1)

    def bands(s, i):
        if xor and s >= near:
            return (fbh, fbl)[i], s - near
        return (nbh, nbl)[i], s

    blank = jnp.zeros((2, 16, 2 * LANES), BF16)
    for ref in (vh, vl):
        ref[0:2] = blank
        ref[pairs + 2 : pairs + 4] = blank
    inside = where.inside()

    acc[0 : near * 8 + 4] = nacc[...]
    if ntiles:
        acc[near * 8 + 4 :] = jnp.zeros((pairs - near * 8, 16, 2 * LANES), F32)
        blocks = [where.block(near + k) - near for k in range(len(tiles))]
        high, low, _ = tables(taps_ref, radius_ref)
        lines = [halo[halo.shape[0] - 1, 8 + j : 9 + j, :] for j in range(ntiles)]
        make_bands(where, blocks, high, low, lines, halo, base_ref, fbh, fbl)
        make_window(where, blocks, tiles, halo, uh, ul)
        for s in range(near, rows):
            spread_rows(bands, uh, ul, near, acc, s)

    def finish(n, count):
        def body(s):
            start = s * 8
            value = acc[pl.ds(start + 2, 8)]
            if n > 0:
                value = value - shift * kr[n - 1, pl.ds(start, 8)]
            value = value * inside[None]
            kr[n, pl.ds(start, 8)] = value
            high, low = split(value)
            vh[pl.ds(start + 2, 8)] = high
            vl[pl.ds(start + 2, 8)] = low

        where.each(body, count)

    def forward(first, count, last):
        def body(s):
            total = gather_rows(bands, vh, vl, s)
            if last:
                kr[NB - 1, pl.ds(s * 8, 8)] = total
            for ref, value in zip((uh, ul), split(total)):
                ref[pl.ds(s * 8, 8)] = value

        where.each(body, count, first)

    fewer = rows - 1
    finish(0, rows)
    for n, first, into, out in ((1, 1, rows, rows), (2, 0, fewer, fewer)):
        forward(first, into, False)
        if n == 1 and xor:
            acc[0:12] = nacc1[...]
            acc[12:] = jnp.zeros((pairs - 8, 16, 2 * LANES), F32)
        else:
            acc[...] = jnp.zeros_like(acc)
        where.each(lambda s: spread_rows(bands, uh, ul, 0, acc, s), into, first)
        finish(n, out)
    for ref, row in zip((keep_ref, send_ref), where.own()):
        for n in range(NB - 1):
            for p in range(8):
                ref[n, p] = halves(kr[n, row * 8 + p])
    gram, blank = jnp.zeros((NB * 16, NB * 16), F32), jnp.zeros((16, 2 * LANES), F32)
    for p in range(8):
        stack = [jnp.concatenate([ref[n, p] for n in range(NB - 1)], 0) for ref in (keep_ref, send_ref)]
        gram = gram + exact_gram(jnp.concatenate([jnp.concatenate(stack, 1), blank], 0))
    gram = jnp.concatenate([gram, jnp.zeros_like(gram)], 1)
    forward(0, fewer, True)
    final = jnp.zeros((16, 16), F32)
    mine, pair = where.own()
    for p in range(8):
        stack = [halves(kr[NB - 1, row * 8 + p]) for row in (mine, pair)]
        final = final + exact_gram(jnp.concatenate(stack, 1))
    extra[...] = jnp.zeros_like(extra)
    extra[:, :16] = final
    lanes, sub = lane_iota(16), lax.broadcasted_iota(jnp.int32, (16, LANES), 0)
    rel = lanes & 15

    def moved(i, j, a):
        return pltpu.roll(gram[16 * i : 16 * i + 16], (16 * (a - j)) % LANES, 1)

    message = jnp.zeros((16, LANES), F32)
    for a in range(NB - 1):
        even = moved(a, a, a)
        odd = moved(a, a + 1, a) if a < NB - 2 else pltpu.roll(extra[...], 16 * a, 1) - shift[:, :LANES] * even
        here = lanes >> 4 == a
        message = jnp.where(here, jnp.where(sub >= rel, even, odd), message)
        corner = jnp.sum(jnp.where(here & (sub == rel), odd, 0.0), axis=1, keepdims=True)
        message = jnp.where(lanes == 48 + a, corner, message)
    message = jnp.where(lanes[:8] < LANES // 2, message[:8], pltpu.roll(message[8:], LANES // 2, 1))
    share = copies.shape[0]
    for dev in range(share):
        copies[dev] = message
    moves = [
        pltpu.make_async_copy(copies, gram_ref.at[pl.ds(i * share, share)], sems.at[i])
        for i in range(ndev // share)
    ]
    for move in moves:
        move.start()
    for move in moves:
        move.wait()


def last_kernel(rows, xor, real_ref, nbh, nbl, fbh, fbl, uh, ul, keep_ref, send_ref, keep3, send3, acc):
    where = Rows(rows, xor)
    near = nbh.shape[0]
    acc[...] = jnp.zeros_like(acc)
    bands = lambda s, i: ((nbh, nbl)[i], s)
    where.each(lambda s: spread_rows(bands, uh, ul, 0, acc, s), near)
    if xor:
        wh, wl = (stage_weights(ref, 0, True) for ref in (fbh, fbl))
        high = uh[near * 8 : near * 8 + 2].reshape(32, 2 * LANES)
        low = ul[near * 8 : near * 8 + 2].reshape(32, 2 * LANES)
        for t in (3, 4):
            out = product(high, low, wh[t], wl[t], NN).reshape(2, 16, 2 * LANES)
            acc[near * 8 + 4 - t : near * 8 + 6 - t] += out
    for ref, old, row in zip((keep3, send3), (keep_ref, send_ref), where.own()):
        for p in range(8):
            ref[p] = halves(acc[row * 8 + 2 + p]) - real_ref[0:1, :] * old[NB - 2, p]


def final_kernel(
    ndev, xor, real_ref, gram_ref, keep_ref, keep3, other_ref, other3, solution_ref, residual_ref
):
    r, q, _ = place()
    damp = real_ref[0:1, :] + 0.25 * DAMPING
    parts = [gram_ref[dev] for dev in range(ndev)]
    while len(parts) > 1:
        parts = [a + b for a, b in zip(parts[::2], parts[1::2])]
    lanes, sub = lane_iota(16), lax.broadcasted_iota(jnp.int32, (16, LANES), 0)
    shared = jnp.concatenate([parts[0], pltpu.roll(parts[0], LANES // 2, 1)], 0)
    turned = jnp.concatenate([shared] + [jnp.zeros_like(shared)] * 7, 0).T
    grams = []
    for a in range(NB - 1):
        block = pltpu.roll(shared, LANES - 16 * a, 1) if a else shared
        other = turned[16 * a : 16 * a + 16]
        corner = shared[:, 48 + a : 49 + a]
        grams.append(jnp.where(sub >= lanes, block, other))
        grams.append(jnp.where(sub < lanes, block, jnp.where(sub == lanes, corner, other)))

    def at(g, place):
        return pltpu.roll(grams[g], 16 * place, 1) if place else grams[g]

    def line_of(entry):
        line = jnp.zeros((16, LANES), F32)
        for j in range(3):
            line = jnp.where(lanes >> 4 == j, entry(j), line)
        return line

    lines = [line_of(lambda j: at(i + j + 1, j) + damp * at(i + j, j)) for i in range(3)]
    matrix = jnp.concatenate(lines + [line_of(lambda j: at(j, j))], 0)
    lane = lane_iota(64)
    for panel in range(6):
        spread = [
            jnp.broadcast_to(matrix[:, 8 * panel + i : 8 * panel + i + 1], (64, LANES)) for i in range(8)
        ]
        for i in range(8):
            k = 8 * panel + i
            column = spread[i]
            scaled = column * (1.0 / column[k : k + 1, :])
            matrix = jnp.where(lane == k, scaled, matrix - scaled * matrix[k : k + 1, :])
            for j in range(i + 1, 8):
                m = 8 * panel + j
                spread[j] = spread[j] - scaled * column[m : m + 1, :]
    c = jnp.where(lanes < 48, matrix[48:], 0.0)
    eye = (sub == lanes).astype(F32)
    weights = jnp.concatenate([0.5 * c, 2.0 * (eye - damp * c - pltpu.roll(c, 16, 1))], 0)[:, : NB * 16]
    weights = exact_weights(weights)
    down = r >> 1
    first = lanes < LANES // 2
    first2 = jnp.concatenate([first, first], 0)
    outs = (
        solution_ref.reshape(16 * SUB, LANES),
        residual_ref.reshape(16 * SUB, LANES),
    )
    for p in range(8):
        at = p + down * (7 - 2 * p) if xor else p
        mine = jnp.concatenate([keep_ref[n, at] for n in range(NB - 1)] + [keep3[at]], 0)
        pair = jnp.concatenate([other_ref[n, at] for n in range(NB - 1)] + [other3[at]], 0)
        both = jnp.concatenate([mine, pair], 1)
        out = exact_combination(weights, both)
        a, b = out[:, :LANES], out[:, LANES:]
        left, right = jnp.where(q == 0, a, b), jnp.where(q == 0, b, a)
        even = jnp.where(first2, left, pltpu.roll(right, LANES // 2, 1))
        odd = jnp.where(first2, pltpu.roll(left, LANES // 2, 1), right)
        if xor:
            even, odd = jnp.where(down > 0, odd, even), jnp.where(down > 0, even, odd)
        for i, line in ((2 * p, even), (2 * p + 1, odd)):
            for o, ref in enumerate(outs):
                ref[pl.ds(i, 16, stride=SUB), :] = line[16 * o : 16 * o + 16]


def per_device(measured, regions, kernels, radius):
    nrow, ncol = lax.axis_size("row"), lax.axis_size("col")
    ndev = nrow * ncol
    def flip(value, bit):
        return lax.ppermute(value, "row", [(i, i ^ bit) for i in range(nrow)])

    facing = []
    for i in range(nrow):
        for j in range(ncol):
            other = j + (1 if (i ^ j) & 1 else -1)
            if 0 <= other < ncol:
                facing.append((i * ncol + j, i * ncol + other))

    def call(kernel, name, out, operands, scratch, mib, specs=None):
        return pl.pallas_call(
            kernel,
            out_shape=[jax.ShapeDtypeStruct(shape, kind) for shape, kind in out],
            in_specs=[VMEM] * len(operands),
            out_specs=specs or [VMEM] * len(out),
            scratch_shapes=[pltpu.VMEM(*s) if isinstance(s, tuple) else s for s in scratch],
            compiler_params=params(mib),
            name=name,
        )(*operands)

    def bands_of(count):
        return ((count, K, LANES, LANES), BF16)

    def rows_of(count, kind):
        return ((count, 16, 2 * LANES), kind)

    def bases_of(count):
        return ((count, K, 8, LANES), F32)

    def edges_of(count):
        return ((count * (SUB // PACK), 16, LANES), F32)

    xor = nrow == 4
    if xor:
        mine = measured[None]
        tiles = [mine, flip(mine, 1)]
        labels = [regions, flip(regions, 1)]
        over = flip(mine, 2)
    else:
        tiles = [lax.all_gather(measured, "row", axis=0)]
        labels = [lax.all_gather(regions, "row", axis=0, tiled=True)]
    near, pairs = sum(t.shape[0] for t in tiles), nrow * SUB // 2
    edges, reach = call(
        first_kernel,
        "first",
        [edges_of(tiles[0].shape[0]), ((8, LANES), jnp.int32)],
        [tiles[0], radius[None]],
        [],
        4,
    )
    slots = edges_of(near)[0][0] + 1
    edges, tags = call(
        functools.partial(pack_kernel, len(labels)),
        "pack",
        [((slots, 16, LANES), F32), ((16, LANES), F32)],
        [edges, *labels, *tiles[1:]],
        [],
        4,
    )
    halo = lax.ppermute(edges, ("row", "col"), facing)
    taps = jnp.transpose(kernels, (1, 2, 0))
    nbh, nbl, nacc, nacc1, real = call(
        functools.partial(near_kernel, nrow, xor, len(tiles)),
        "near",
        [bands_of(near)] * 2 + [rows_of(near * 8 + 4, F32), rows_of(12, F32), ((8, LANES), F32)],
        [taps, reach, tags, halo, *tiles],
        [bases_of(near)] + [rows_of(near * 8, BF16)] * 2 + [rows_of(12, BF16)] * 2,
        8 + 2 * nrow,
    )
    far, ntiles = [], 0
    if xor:
        over, halo = lax.optimization_barrier((over, halo))
        (joined,) = call(join_kernel, "join", [((slots, 16, LANES), F32)], [halo, tags], [], 4)
        far, ntiles = [flip(joined, 2), over, flip(over, 1)], 2
    packed = ((NB - 1, 8, 16, LANES), F32)
    extra = max(nrow - near, 1)
    share = max(ndev // 8, 1)
    out = [((ndev, 8, LANES), F32), packed, packed] + [rows_of(pairs, BF16)] * 2 + [bands_of(extra)] * 2
    grams, keep, send, uh, ul, fbh, fbl = call(
        functools.partial(main_kernel, nrow, xor, ndev, ntiles),
        "krylov",
        out,
        [taps, reach, real, nbh, nbl, nacc, nacc1, *far],
        [bases_of(extra)]
        + [rows_of(pairs + 4, BF16)] * 2
        + [rows_of(pairs + 4, F32), ((NB, pairs, 16, 2 * LANES), F32), ((16, LANES), F32)]
        + [((share, 8, LANES), F32), pltpu.SemaphoreType.DMA((ndev // share,))],
        8 + 3 * nrow,
        [pl.BlockSpec(memory_space=pl.ANY)] + [VMEM] * (len(out) - 1),
    )
    grams = lax.all_to_all(grams, ("row", "col"), 0, 0)
    single = ((8, 16, LANES), F32)
    keep3, send3 = call(
        functools.partial(last_kernel, nrow, xor),
        "last",
        [single, single],
        [real, nbh, nbl, fbh, fbl, uh, ul, keep, send],
        [rows_of(near * 8 + 4, F32)],
        8 + 2 * nrow,
    )
    send, send3 = lax.optimization_barrier((send, send3))
    tile = ((16, SUB, LANES), F32)
    return tuple(
        call(
            functools.partial(final_kernel, ndev, xor),
            "combine",
            [tile, tile],
            [real, grams, keep, keep3, flip(send, 1), flip(send3, 1)],
            [],
            8,
        )
    )


def solution(mesh):
    in_specs = (P(None, "row", "col"), P("row", "col"), P(), P())
    out_specs = (P(None, "row", "col"), P(None, "row", "col"))
    return jax.shard_map(
        per_device, mesh=mesh, in_specs=in_specs, out_specs=out_specs, check_vma=False
    )
```
